32 devices in a mesh: seq: 4 (over x, core), fsdp: 8 (over z, y).
Axes of the slice: x: 2, y: 2, z: 4, core: 2. Of those that a mesh axis runs over, the one named last changes fastest.
Arguments:
- inputs: bfloat16 [8, 1024, 512], P('fsdp', 'seq'), may hold values from -6 to 6
- block_ids: int32 [8, 1024], P('fsdp'), may hold values from 0 to 7, never falling along the last dimension, each value on 1 to 256 neighbouring positions
- query_weight: bfloat16 [512, 512], P('fsdp'), may hold values from -0.25 to 0.25
- query_bias: bfloat16 [512], P('fsdp'), may hold values from -1.5 to 1.5
- key_weight: bfloat16 [512, 512], P('fsdp'), may hold values from -0.25 to 0.25
- value_weight: bfloat16 [512, 512], P('fsdp'), may hold values from -0.25 to 0.25
- value_bias: bfloat16 [512], P('fsdp'), may hold values from -1.5 to 1.5
- out_weight: bfloat16 [512, 512], P('fsdp'), may hold values from -6 to 6
- out_bias: bfloat16 [512], P('fsdp'), may hold values from -1.5 to 1.5
- gain_one: bfloat16 [512], P('fsdp'), may hold values from 0.5 to 1.5
- shift_one: bfloat16 [512], P('fsdp'), may hold values from -1.5 to 1.5
- up_weight: bfloat16 [512, 2048], P('fsdp'), may hold values from -0.25 to 0.25
- up_bias: bfloat16 [2048], P('fsdp'), may hold values from -1.5 to 1.5
- down_weight: bfloat16 [2048, 512], P('fsdp'), may hold values from -0.125 to 0.125
- down_bias: bfloat16 [512], P('fsdp'), may hold values from -1.5 to 1.5
- gain_two: bfloat16 [512], P('fsdp'), may hold values from 0.5 to 1.5
- shift_two: bfloat16 [512], P('fsdp'), may hold values from -1.5 to 1.5
- cotangent: bfloat16 [8, 1024, 512], P('fsdp', 'seq'), may hold values from -6 to 6
Outputs:
- output: bfloat16 [8, 1024, 512], P('fsdp', 'seq')
- input_grad: float32 [8, 1024, 512], P('fsdp', 'seq')
- query_weight_grad: float32 [512, 512], P('fsdp')
- query_bias_grad: float32 [512], P('fsdp')
- key_weight_grad: float32 [512, 512], P('fsdp')
- value_weight_grad: float32 [512, 512], P('fsdp')
- value_bias_grad: float32 [512], P('fsdp')
- out_weight_grad: float32 [512, 512], P('fsdp')
- out_bias_grad: float32 [512], P('fsdp')
- gain_one_grad: float32 [512], P('fsdp')
- shift_one_grad: float32 [512], P('fsdp')
- up_weight_grad: float32 [512, 2048], P('fsdp')
- up_bias_grad: float32 [2048], P('fsdp')
- down_weight_grad: float32 [2048, 512], P('fsdp')
- down_bias_grad: float32 [512], P('fsdp')
- gain_two_grad: float32 [512], P('fsdp')
- shift_two_grad: float32 [512], P('fsdp')
The draws below stay inside these ranges and needn't reach their ends.
Inputs may be any that keep to these rules, and one draw needn't show every extreme that they name: `block_ids`: in each sequence the block numbers never fall along the positions, every number from 0 to 7 occurs, each block spans at most 256 positions, and in every draw some block spans exactly 256.
All inputs are finite; a program needn't handle non-finite values.
Results may differ from the reference program's by a relative error of at most 0.019.
Values may be sent and summed in bfloat16 or wider, within the bound.
No kernel may reach another device: no remote copies, remote signals or barrier semaphores. Data moves between devices by JAX's collectives and lax.ppermute only.
A program may use at most 128 MiB of HBM per device.

```python
import math
import jax
import jax.numpy as jnp
import numpy as np
from jax import lax

D = 512
H = 8
DH = 64
FF = 2048
SEQ_POS = 1
BLOCK = 256
LEN = 1024
NBLK = 8
SEQS = 8
N_FSDP = 8


def raised(values, rng, source, target, blocks, factor):
    def block_of(dim):
        return (jnp.arange(values.shape[dim]) // (values.shape[dim] // blocks)).reshape((-1,) + (1,) * (values.ndim - 1 - dim))

    first = jax.random.permutation(rng, blocks)[block_of(target)]
    second = (block_of(target) + blocks // 2) % blocks
    return jnp.where((block_of(source) == first) | (block_of(source) == second), factor * values, values)


def block_levels(own_key, extent, shards, low, high):
    def one(axis_at, shards_of):
        heights = jax.random.uniform(jax.random.fold_in(jax.random.fold_in(own_key, 6), axis_at), (shards_of,), jnp.float32, low / len(shards), high / len(shards))
        return jnp.repeat(jnp.exp(heights), extent[axis_at] // shards_of).reshape((-1,) + (1,) * (len(extent) - axis_at - 1))

    loudness = one(*shards[0])
    for cut in shards[1:]:
        loudness = loudness * one(*cut)
    return loudness


def split_up(amount, total, most, slope):
    portions = [(1 << 20) // math.isqrt(rank ** slope) + 1 for rank in range(2, amount + 1)]
    spare, holding = total - most - (amount - 1), [1] * (amount - 1)
    while spare > 0:
        movable = [i for i in range(amount - 1) if holding[i] < most]
        whole, left = sum([portions[i] for i in movable]), spare
        for i in movable:
            addition = min(most - holding[i], max(1, left * portions[i] // whole), spare)
            holding[i] = holding[i] + addition
            spare = spare - addition
    return np.array([most] + holding)


def uneven_parts(key, number_of, total, limit, slope):
    if number_of == 2:
        one = jax.random.randint(key, (), max(1, total - limit), min(limit, total - 1) + 1)
        return jnp.stack([one, total - one])
    lengths = jnp.asarray(split_up(number_of, total, limit, slope), jnp.int32)
    twos = (number_of - 1) // 2
    donor, taker = lengths[1:1 + 2 * twos:2], lengths[2:2 + 2 * twos:2]
    margin = jnp.minimum(donor - 1, limit - taker)
    shifted = jax.random.randint(jax.random.fold_in(key, 1), (twos,), 0, 1 << 20) % (margin + 1)
    lengths = lengths.at[1:1 + 2 * twos:2].set(donor - shifted).at[2:2 + 2 * twos:2].set(taker + shifted)
    return lengths[jax.random.permutation(jax.random.fold_in(key, 2), number_of)]


def gaussian(rng, shape, scale, reach, pieces=(), kind=jnp.bfloat16):
    array = jax.random.normal(rng, shape, jnp.float32) * scale
    if len(pieces) > 0:
        array = block_levels(rng, shape, pieces, -0.22, 0.18) * array
    return jnp.clip(array, min=-reach, max=reach).astype(kind)


def bell_draw_with(stream_key, dims, deviation, limit, cuts, heavy, kind=jnp.bfloat16):
    entries = deviation * jax.random.normal(stream_key, dims, jnp.float32)
    if cuts:
        entries = entries * block_levels(stream_key, dims, cuts, -0.22, 0.18)
    return jnp.clip(raised(entries, jax.random.fold_in(stream_key, 3), *heavy), -limit, limit).astype(kind)


def setup_inputs(seed: int = 0) -> dict:
    key_of = jax.random.split(jax.random.key(seed), 19)
    return {
        "inputs": bell_draw_with(key_of[0], (SEQS, LEN, D), 1.0, 6.0, ((0, 8), (1, 4)), (0, 2, 8, 2.0)),
        "block_ids": jax.vmap(lambda own: jnp.searchsorted(jnp.cumsum(uneven_parts(own, NBLK, LEN, BLOCK, 0)), jnp.arange(LEN), side="right"))(jax.random.split(key_of[1], SEQS)).reshape((SEQS, LEN)).astype(jnp.int32),
        "query_weight": gaussian(key_of[2], (D, D), D ** -0.5, 0.25, ((0, 8),)),
        "query_bias": gaussian(key_of[3], (D,), 0.3, 1.5, ((0, 8),)),
        "key_weight": gaussian(key_of[4], (D, D), D ** -0.5, 0.25, ((0, 8),)),
        "value_weight": gaussian(key_of[5], (D, D), D ** -0.5, 0.25, ((0, 8),)),
        "value_bias": gaussian(key_of[6], (D,), 0.3, 1.5, ((0, 8),)),
        "out_weight": gaussian(key_of[7], (D, D), (max(2 * D // LEN, 1)) ** -0.5, 6.0, ((0, 8),)),
        "out_bias": gaussian(key_of[8], (D,), 0.3, 1.5, ((0, 8),)),
        "gain_one": jnp.clip(1.0 + 0.1 * jax.random.normal(key_of[9], (D,), jnp.float32), 0.5, 1.5).astype(jnp.bfloat16),
        "shift_one": gaussian(key_of[10], (D,), 0.3, 1.5, ((0, 8),)),
        "up_weight": gaussian(key_of[11], (D, FF), D ** -0.5, 0.25, ((0, 8),)),
        "up_bias": gaussian(key_of[12], (FF,), 0.3, 1.5, ((0, 8),)),
        "down_weight": gaussian(key_of[13], (FF, D), FF ** -0.5, 0.125, ((0, 8),)),
        "down_bias": gaussian(key_of[14], (D,), 0.3, 1.5, ((0, 8),)),
        "gain_two": jnp.clip(1.0 + 0.1 * jax.random.normal(key_of[15], (D,), jnp.float32), 0.5, 1.5).astype(jnp.bfloat16),
        "shift_two": gaussian(key_of[16], (D,), 0.3, 1.5, ((0, 8),)),
        "cotangent": bell_draw_with(key_of[17], (SEQS, LEN, D), 1.0, 6.0, ((0, 8), (1, 4)), (0, 2, 8, 2.0)),
    }


@jax.custom_vjp
def low(v):
    return lax.optimization_barrier(v.astype(jnp.bfloat16)).astype(jnp.float32)

@jax.custom_vjp
def low_back(v):
    return v

def low_keep(v):
    return (low(v), None)

def low_pass(kept, grad):
    return (grad,)

def back_keep(v):
    return (v, None)

def back_low(kept, grad):
    return (low(grad),)
low.defvjp(low_keep, low_pass)
low_back.defvjp(back_keep, back_low)
norm_eps = 1e-05
masked_score = -1e+30

def matmul(left, right):
    return jnp.dot(left, right, precision=lax.Precision.HIGHEST, preferred_element_type=jnp.float32)

def layer_norm(summed, gain, shift):
    centre = summed - lax.optimization_barrier(jnp.mean(summed, axis=-1, keepdims=True))
    scaled = centre * lax.rsqrt(lax.optimization_barrier(jnp.mean(centre * centre, axis=-1, keepdims=True)) + norm_eps)
    return scaled * gain + shift

def attend_head(query_head, key_head, value_head, blocks):
    scores = jnp.dot(query_head, key_head.T, precision=lax.Precision.HIGHEST)
    scores = low_back(scores * (1.0 / math.sqrt(DH)))
    allowed = blocks[None, :] <= blocks[:, None]
    scores = jnp.where(allowed, scores, masked_score)
    probs = low(jax.nn.softmax(scores, axis=-1))
    return jnp.dot(probs, value_head, precision=lax.Precision.HIGHEST)

def attend(queries, key_rows, value_rows, blocks):
    length = queries.shape[0]
    query_heads = jnp.transpose(queries.reshape(length, H, DH), (1, 0, 2))
    key_heads = jnp.transpose(key_rows.reshape(length, H, DH), (1, 0, 2))
    value_heads = jnp.transpose(value_rows.reshape(length, H, DH), (1, 0, 2))
    step = jax.checkpoint(lambda items: attend_head(items[0], items[1], items[2], blocks))
    mixed = lax.map(step, (query_heads, key_heads, value_heads))
    return jnp.transpose(mixed, (1, 0, 2)).reshape(length, H * DH)

def forward(inputs, params, blocks):
    query_weight, query_bias, key_weight, value_weight, value_bias, out_weight, out_bias, gain_one, shift_one, up_weight, up_bias, down_weight, down_bias, gain_two, shift_two = params
    token_rows = inputs.reshape(-1, D)
    queries = low_back(low(matmul(token_rows, query_weight) + query_bias))
    key_rows = low_back(low(matmul(token_rows, key_weight)))
    value_rows = low_back(low(matmul(token_rows, value_weight) + value_bias))
    step = jax.checkpoint(lambda items: attend(items[0], items[1], items[2], items[3]))
    mixed = lax.map(step, (queries.reshape(-1, LEN, D), key_rows.reshape(-1, LEN, D), value_rows.reshape(-1, LEN, D), blocks))
    mixed_rows = low_back(low(mixed.reshape(-1, D)))
    attention = low_back(matmul(mixed_rows, out_weight) + out_bias)
    first = low(layer_norm(token_rows + attention, gain_one, shift_one))
    up_out = low_back(matmul(first, up_weight) + up_bias)
    hidden = low_back(low(jax.nn.gelu(up_out, approximate=True)))
    branch = low_back(matmul(hidden, down_weight) + down_bias)
    return layer_norm(first + branch, gain_two, shift_two).reshape(inputs.shape)

def reference(inputs, block_ids, query_weight, query_bias, key_weight, value_weight, value_bias, out_weight, out_bias, gain_one, shift_one, up_weight, up_bias, down_weight, down_bias, gain_two, shift_two, cotangent):
    params = tuple((item.astype(jnp.float32) for item in (query_weight, query_bias, key_weight, value_weight, value_bias, out_weight, out_bias, gain_one, shift_one, up_weight, up_bias, down_weight, down_bias, gain_two, shift_two)))
    group_inputs = inputs.astype(jnp.float32).reshape(N_FSDP, SEQ_POS, LEN, D)
    group_cotangent = cotangent.astype(jnp.float32).reshape(N_FSDP, SEQ_POS, LEN, D)
    group_blocks = block_ids.reshape(N_FSDP, SEQ_POS, LEN)

    def one_group(totals, group):
        seg_inputs, seg_cotangent, seg_blocks = group

        def local(values, weights):
            return forward(values, weights, seg_blocks)
        result, pullback = jax.vjp(local, seg_inputs, params)
        grad_inputs, grad_params = pullback(seg_cotangent)
        totals = jax.tree.map(jnp.add, totals, grad_params)
        return (totals, (result.astype(jnp.bfloat16), grad_inputs))
    start = jax.tree.map(jnp.zeros_like, params)
    totals, (results, grad_inputs) = lax.scan(one_group, start, (group_inputs, group_cotangent, group_blocks))
    return (results.reshape(SEQS, LEN, D), grad_inputs.reshape(SEQS, LEN, D), totals[0], totals[1], totals[2], totals[3], totals[4], totals[5], totals[6], totals[7], totals[8], totals[9], totals[10], totals[11], totals[12], totals[13], totals[14])
```

```python
import functools
import math

import jax
import jax.numpy as jnp
from jax import lax
from jax.experimental import pallas as pl
from jax.experimental.pallas import tpu as pltpu
from jax.sharding import PartitionSpec as P

HEADS = 8
BLOCKS = 8
PARTS = 8
NORM_EPS = 1e-05
MASKED = -1e30
GELU_ROOT = 0.7978845608028654
GELU_CUBIC = 0.044715
BF = jnp.bfloat16
F32 = jnp.float32
VMEM = pl.BlockSpec(memory_space=pltpu.VMEM)
SMEM = pl.BlockSpec(memory_space=pltpu.SMEM)


def dot_nn(left, right):
    return lax.dot_general(left, right, (((1,), (0,)), ((), ())), preferred_element_type=F32)


def dot_nt(left, right):
    return lax.dot_general(left, right, (((1,), (1,)), ((), ())), preferred_element_type=F32)


def dot_tn(left, right):
    return lax.dot_general(left, right, (((0,), (0,)), ((), ())), preferred_element_type=F32)


def run(kernel, outs, index, args, scratch=(), flops=0, moved=0):
    outs = [jax.ShapeDtypeStruct(*o) for o in outs]
    return pl.pallas_call(
        kernel,
        out_shape=outs,
        in_specs=[SMEM] + [VMEM] * len(args),
        out_specs=[VMEM] * len(outs),
        scratch_shapes=[pltpu.VMEM(*s) for s in scratch],
        compiler_params=pltpu.CompilerParams(vmem_limit_bytes=56 * 1024 * 1024),
        cost_estimate=pl.CostEstimate(flops=flops, bytes_accessed=moved, transcendentals=0),
    )(index, *args)


def lanes_of(shape):
    return lax.broadcasted_iota(jnp.int32, shape, len(shape) - 1)


def rows_of(shape):
    return lax.broadcasted_iota(jnp.int32, shape, len(shape) - 2)


def half_roll(values):
    return pltpu.roll(values, 64, 1)


def pack_kernel(idx, wq, wk, wv, wo, up, down, vec, head_out, up_out, down_out):
    s, c = idx[1], idx[2]
    columns = pl.ds(pl.multiple_of(s * 128, 128), 128)
    for i, ref in enumerate((wq, wk, wv)):
        head_out[:64, i * 128 : (i + 1) * 128] = ref[:, columns]
    head_out[64:80, :] = vec[...]
    rows = pl.ds(pl.multiple_of(c * 32, 32), 32)
    up_out[:, :512] = wo[rows, :]
    up_out[:, 512:] = up[rows, :]
    down_out[...] = down[pl.ds(pl.multiple_of(c * 128, 128), 128), :]


def stack_kernel(idx, a, b, c, d, out):
    for i, ref in enumerate((a, b, c, d)):
        out[i] = ref[...]


def load_vectors(idx, parts, first, second):
    f = idx[0]
    for k, ref in enumerate(parts):
        rows = ref[64:80, :].astype(F32)
        first[pl.ds(f ^ k, 1), :] = rows[0:1]
        second[pl.ds(f ^ k, 1), :] = rows[1:2]


def load_heads(idx, parts, weight):
    f = idx[0]
    for k, ref in enumerate(parts):
        weight[pl.ds(pl.multiple_of((f ^ k) * 64, 64), 64), :] = ref[:64, :]


def key_limit(i, part, count):
    return min((i + 2) * part, count * part)


def attend_kernel(idx, *refs):
    xs, parts, ids = refs[:4], refs[4:12], refs[12]
    ms = refs[13:17]
    qa, ka, v_out, m_out, rinv_out = refs[17:22]
    weight, first, second, q_s, k_s = refs[22:]
    s = idx[1]
    part = xs[0].shape[0]
    count = ids.shape[1] // part
    total = part * count
    load_heads(idx, parts, weight)
    load_vectors(idx, parts, first, second)
    even, odd = first[pl.ds(2 * s, 1), :][:, :128], first[pl.ds(2 * s + 1, 1), :][:, :128]
    low_row = lanes_of((1, 128)) < 64
    query_bias = jnp.where(low_row, even, half_roll(odd))
    value_bias = jnp.where(low_row, half_roll(even), odd)
    for k, ref in enumerate(xs):
        rows = pl.ds(pl.multiple_of((s ^ k) * part, part), part)
        made = dot_nn(ref[...], weight[...])
        q_s[rows, :] = (made[:, :128] + query_bias).astype(BF)
        k_s[rows, :] = made[:, 128:256].astype(BF)
        v_out[rows, :] = (made[:, 256:] + value_bias).astype(BF)
    blocks = jnp.broadcast_to(ids[...], (128, total))
    row = rows_of((128, total))
    row = jnp.where(row >= 64, row - 64, row)
    own = jnp.where((row < BLOCKS) & (blocks == row), 1.0, 0.0).astype(F32).T
    barred = jnp.where(
        row < BLOCKS,
        jnp.where(blocks > row, MASKED, 0.0),
        jnp.where(row < BLOCKS + 3, 1.0, 0.0),
    ).astype(F32).T
    lane = lanes_of((total, 128))
    low = lane < 64
    queries = q_s[...].astype(F32) * (1.0 / math.sqrt(64))
    keys = k_s[...].astype(F32)
    qa[0] = jnp.where(low, queries, own).astype(BF)
    qa[1] = jnp.where(low, own, queries).astype(BF)
    ka[0] = jnp.where(low, keys, barred).astype(BF)
    ka[1] = jnp.where(low, barred, keys).astype(BF)
    lane = lanes_of((part, 128))
    low = lane < 64
    for i in range(count):
        rows = slice(i * part, (i + 1) * part)
        limit = key_limit(i, part, count)
        mixed = []
        sums = []
        for h in range(2):
            scores = dot_nt(qa[h, rows, :], ka[h, :limit, :])
            top = jnp.max(scores, axis=-1, keepdims=True)
            raised = jnp.exp(scores - top).astype(BF)
            values = v_out[:limit, :]
            mine = lanes_of(values.shape) < 64
            values = jnp.where(mine if h == 0 else ~mine, values, jnp.ones_like(values))
            made = dot_nn(raised, values)
            sums.append(1.0 / half_roll(made))
            mixed.append(made * sums[-1])
            high = top.astype(BF).astype(F32)
            middle = (top - high).astype(BF).astype(F32)
            rest = top - high - middle
            at = lane - (64 if h == 0 else 0) - BLOCKS
            tops = jnp.where(at == 0, -high, jnp.where(at == 1, -middle, jnp.where(at == 2, -rest, 0.0)))
            held = qa[h, rows, :].astype(F32)
            qa[h, rows, :] = jnp.where((at >= 0) & (at < 3), tops, held).astype(BF)
        m_out[rows, :] = jnp.where(low, mixed[0], mixed[1]).astype(BF)
        rinv_out[rows, :] = jnp.where(low, sums[0], sums[1])
    for k, ref in enumerate(ms):
        ref[...] = m_out[pl.ds(pl.multiple_of((s ^ k) * part, part), part), :]


def spread(block, upper, width):
    row = rows_of((PARTS, 128))
    match = (row & 1) == (1 if upper else 0)
    block = jnp.where(match, block, half_roll(block))
    tiled = jnp.concatenate([block] * (width // 128), axis=1)
    keep = lanes_of((PARTS, width)) // 64 == rows_of((PARTS, width))
    return jnp.sum(jnp.where(keep, tiled, 0.0), axis=0, keepdims=True)


def gather_up(vector, upper):
    width = vector.shape[1]
    keep = lanes_of((PARTS, width)) // 64 == rows_of((PARTS, width))
    picked = jnp.where(keep, jnp.broadcast_to(vector, (PARTS, width)), 0.0)
    block = sum(picked[:, j * 128 : (j + 1) * 128] for j in range(width // 128))
    match = (rows_of((PARTS, 128)) & 1) == (1 if upper else 0)
    return jnp.where(match, block, half_roll(block))


def normalize(summed):
    centre = summed - jnp.mean(summed, axis=-1, keepdims=True)
    inverse = lax.rsqrt(jnp.mean(centre * centre, axis=-1, keepdims=True) + NORM_EPS)
    return centre * inverse, inverse


def norm_back(grad, normed, inverse):
    first_mean = jnp.mean(grad, axis=-1, keepdims=True)
    cross_mean = jnp.mean(grad * normed, axis=-1, keepdims=True)
    return inverse * (grad - first_mean - normed * cross_mean)


def gelu(values):
    inner = GELU_ROOT * (values + GELU_CUBIC * values * values * values)
    return 0.5 * values * (1.0 + jnp.tanh(inner))


def gelu_slope(values):
    square = values * values
    inner = GELU_ROOT * (values + GELU_CUBIC * values * square)
    tanh_part = jnp.tanh(inner)
    return 0.5 * (1.0 + tanh_part) + 0.5 * values * (1.0 - tanh_part * tanh_part) * GELU_ROOT * (
        1.0 + 3.0 * GELU_CUBIC * square
    )


def column_sum(values):
    return jnp.sum(values.astype(F32), axis=0, keepdims=True)


def middle_kernel(idx, *refs):
    x0, ms, cot, parts = refs[0], refs[1:5], refs[5], refs[6:14]
    up_parts, down_parts = refs[14:18], refs[18:22]
    refs = refs[22:]
    out, ems, e1_out, u_out, eb_out, y_out, ez_out, m_out, ea_out, vg_out = (
        refs[0],
        refs[1:5],
        *refs[5:13],
    )
    wo, up, down, first, second, z_s, em_s, rows0, rows1 = refs[13:]
    f, s, c = idx[0], idx[1], idx[2]
    for which in range(4):
        half = c if which < 2 else 1 - c
        for j in range(4):
            owner = f ^ (2 * j + (which & 1))
            rows = pl.ds(pl.multiple_of(owner * 64 + half * 32, 32), 32)
            wo[rows, :] = up_parts[which][j, :, :512]
            up[rows, :] = up_parts[which][j, :, 512:]
            rows = pl.ds(pl.multiple_of(owner * 256 + half * 128, 128), 128)
            down[rows, :] = down_parts[which][j]
    load_vectors(idx, parts, first, second)
    v0, v1 = first[...], second[...]
    out_bias = spread(v0[:, 128:256], False, 512)
    gain_one = spread(v0[:, 128:256], True, 512)
    shift_one = spread(v0[:, 256:384], False, 512)
    gain_two = spread(v0[:, 256:384], True, 512)
    shift_two = spread(v1[:, 0:128], False, 512)
    down_bias = spread(v1[:, 0:128], True, 512)
    keep = lanes_of((PARTS, 2048)) // 256 == rows_of((PARTS, 2048))
    tiled = jnp.concatenate([v1[:, 128:384]] * 8, axis=1)
    up_bias = jnp.sum(jnp.where(keep, tiled, 0.0), axis=0, keepdims=True)

    for k, ref in enumerate(ms):
        m_out[:, pl.ds(pl.multiple_of((s ^ k) * 128, 128), 128)] = ref[...]
    h1 = x0[...].astype(F32) + (dot_nn(m_out[...], wo[...]) + out_bias)
    n1, r1 = normalize(h1)
    y = (n1 * gain_one + shift_one).astype(BF)
    y_out[...] = y
    branch = jnp.zeros(h1.shape, F32)
    for j in range(4):
        columns = slice(j * 512, (j + 1) * 512)
        z = dot_nn(y, up[:, columns]) + up_bias[:, columns]
        z_s[:, columns] = z
        u = gelu(z).astype(BF)
        u_out[:, columns] = u
        branch = branch + dot_nn(u, down[columns, :])
    n2, r2 = normalize(y.astype(F32) + (branch + down_bias))
    out[...] = (n2 * gain_two + shift_two).astype(BF)
    grad = cot[...].astype(F32)
    gain_two_grad = column_sum(grad * n2)
    shift_two_grad = column_sum(grad)
    e2 = norm_back(grad * gain_two, n2, r2)
    eb = e2.astype(BF)
    eb_out[...] = eb
    down_bias_grad = column_sum(eb)
    ey = e2
    up_bias_grads = []
    for j in range(4):
        columns = slice(j * 512, (j + 1) * 512)
        eu = dot_nt(eb, down[columns, :]).astype(BF).astype(F32)
        ez = (eu * gelu_slope(z_s[:, columns])).astype(BF)
        ez_out[:, columns] = ez
        up_bias_grads.append(column_sum(ez))
        ey = ey + dot_nt(ez, up[:, columns])
    gain_one_grad = column_sum(ey * n1)
    shift_one_grad = column_sum(ey)
    e1 = norm_back(ey * gain_one, n1, r1)
    e1_out[...] = e1
    ea = e1.astype(BF)
    ea_out[...] = ea
    out_bias_grad = column_sum(ea)
    em_s[...] = dot_nt(ea, wo[...]).astype(BF)
    for k, ref in enumerate(ems):
        ref[...] = em_s[:, pl.ds(pl.multiple_of((s ^ k) * 128, 128), 128)]
    rows0[:, :128] = jnp.zeros((PARTS, 128), F32)
    rows0[:, 128:256] = gather_up(out_bias_grad, False) + gather_up(gain_one_grad, True)
    rows0[:, 256:384] = gather_up(shift_one_grad, False) + gather_up(gain_two_grad, True)
    rows1[:, :128] = gather_up(shift_two_grad, False) + gather_up(down_bias_grad, True)
    up_bias_grad = jnp.concatenate(up_bias_grads, axis=1)
    picked = jnp.where(keep, jnp.broadcast_to(up_bias_grad, (PARTS, 2048)), 0.0)
    rows1[:, 128:384] = sum(picked[:, j * 256 : (j + 1) * 256] for j in range(8))
    at = rows_of((16, 384))
    for k in range(PARTS):
        a, b = rows0[pl.ds(f ^ k, 1), :], rows1[pl.ds(f ^ k, 1), :]
        vg_out[k] = jnp.where(at == 1, a, jnp.where(at == 2, b, 0.0)).astype(BF)


def down_grad_kernel(idx, u, eb, keep, send):
    f, c = idx[0], idx[2]
    right = eb[...]
    for owner in range(PARTS):
        made = dot_tn(u[:, owner * 256 : (owner + 1) * 256], right).astype(BF)
        slot = f ^ owner
        keep[slot] = jnp.where(c == 0, made[:128], made[128:])
        send[slot] = jnp.where(c == 0, made[128:], made[:128])


def up_grad_kernel(idx, y, ez, m, ea, keep, send):
    f, c = idx[0], idx[2]
    for pair in range(PARTS // 2):
        columns = slice(pair * 128, (pair + 1) * 128)
        made_up = dot_tn(y[:, columns], ez[...]).astype(BF)
        made_out = dot_tn(m[:, columns], ea[...]).astype(BF)
        for one in range(2):
            slot = f ^ (2 * pair + one)
            at = one * 64
            for made, lanes in ((made_out, slice(0, 512)), (made_up, slice(512, 2560))):
                upper, lower = made[at : at + 32], made[at + 32 : at + 64]
                keep[slot, :, lanes] = jnp.where(c == 0, upper, lower)
                send[slot, :, lanes] = jnp.where(c == 0, lower, upper)


def attend_back_kernel(idx, *refs):
    ems, qa, ka, v, m, rinv = refs[:4], refs[4], refs[5], refs[6], refs[7], refs[8]
    xs, parts, vg = refs[9:13], refs[13:21], refs[21]
    dx_keep, dx_send, w_keep, w_send = refs[22:26]
    weight, em_s, ema, va, eq_s, e_s, wg_s = refs[26:]
    f, s = idx[0], idx[1]
    part = xs[0].shape[0]
    total = v.shape[0]
    count = total // part
    load_heads(idx, parts, weight)
    for k, ref in enumerate(ems):
        em_s[pl.ds(pl.multiple_of((s ^ k) * part, part), part), :] = ref[...]
    lane = lanes_of((total, 128))
    low = lane < 64
    inverse = rinv[...]
    em = em_s[...].astype(F32)
    scaled = em * inverse
    product = scaled * m[...].astype(F32)
    values = v[...]
    for h in range(2):
        mine = low if h == 0 else ~low
        delta = jnp.sum(jnp.where(mine, product, 0.0), axis=-1, keepdims=True)
        high = delta.astype(BF).astype(F32)
        at = lane - (64 if h == 0 else 0)
        extra = jnp.where(at == 0, -high, jnp.where(at == 1, high - delta, 0.0))
        ema[h] = jnp.where(mine, scaled, extra).astype(BF)
        ones = jnp.where((at == 0) | (at == 1), 1.0, 0.0)
        va[h] = jnp.where(mine, values.astype(F32), ones).astype(BF)
    lane = lanes_of((part, 128))
    low = lane < 64
    eq_s[...] = jnp.zeros_like(eq_s)
    for j in range(count):
        rows = slice(j * part, (j + 1) * part)
        start = max(j - 1, 0) * part
        grad_keys, grad_values = [], []
        for h in range(2):
            raised = jnp.exp(dot_nt(ka[h, rows, :], qa[h, start:, :]))
            slopes = dot_nt(va[h, rows, :], ema[h, start:, :])
            grad = (raised * slopes).astype(BF)
            grad_keys.append(dot_nn(grad, qa[h, start:, :]))
            grad_values.append(dot_nn(raised.astype(BF), ema[h, start:, :]))
            eq_s[h, start:, :] += dot_tn(grad, ka[h, rows, :])
        e_s[rows, 128:256] = jnp.where(low, grad_keys[0], grad_keys[1]).astype(BF)
        e_s[rows, 256:384] = jnp.where(low, grad_values[0], grad_values[1]).astype(BF)
    lane = lanes_of((total, 128))
    e_s[:, :128] = (jnp.where(lane < 64, eq_s[0], eq_s[1]) * (1.0 / math.sqrt(64))).astype(BF)
    wg = jnp.zeros(wg_s.shape, F32)
    for k in range(4):
        grads = e_s[pl.ds(pl.multiple_of((s ^ k) * part, part), part), :]
        wg = wg + dot_tn(xs[k][...], grads)
        made = dot_nt(grads, weight[...]).astype(BF)
        if k & 1:
            dx_send[k >> 1] = made
        else:
            dx_keep[k >> 1] = made
    wg_s[...] = wg
    bias = column_sum(e_s[...])
    at = rows_of((16, 384))
    middle = (lanes_of((16, 384)) >= 128) & (lanes_of((16, 384)) < 256)
    bias = jnp.where((at == 0) & ~middle, jnp.broadcast_to(bias, (16, 384)), 0.0)
    for k in range(PARTS):
        to = w_send if k & 1 else w_keep
        rows = pl.ds(pl.multiple_of((f ^ k) * 64, 64), 64)
        to[k >> 1, :64, :] = wg_s[rows, :].astype(BF)
        to[k >> 1, 64:80, :] = (vg[k].astype(F32) + bias).astype(BF)


def core_sum_kernel(idx, keep, got, stay, go):
    for k in range(PARTS):
        to = go if k & 1 else stay
        to[k >> 1] = (keep[k].astype(F32) + got[k].astype(F32)).astype(BF)


def y_sum_kernel(idx, keep, got, *outs):
    for k in range(PARTS // 2):
        outs[k][...] = (keep[k].astype(F32) + got[k].astype(F32)).astype(BF)


def z_sum_kernel(idx, a, b, c, d, out):
    out[...] = (
        (a[...].astype(F32) + b[...].astype(F32)) + (c[...].astype(F32) + d[...].astype(F32))
    ).astype(BF)


def end_up_kernel(idx, a, b, c, d, out_grad, up_grad):
    core = idx[2]
    own = a[...].astype(F32) + c[...].astype(F32)
    other = b[...].astype(F32) + d[...].astype(F32)
    upper, lower = jnp.where(core == 0, own, other), jnp.where(core == 0, other, own)
    out_grad[:32], out_grad[32:] = upper[:, :512], lower[:, :512]
    up_grad[:32], up_grad[32:] = upper[:, 512:], lower[:, 512:]


def end_down_kernel(idx, a, b, c, d, down_grad):
    core = idx[2]
    own = a[...].astype(F32) + c[...].astype(F32)
    other = b[...].astype(F32) + d[...].astype(F32)
    down_grad[:128] = jnp.where(core == 0, own, other)
    down_grad[128:] = jnp.where(core == 0, other, own)


def end_heads_kernel(idx, a, b, c, d, wq, wk, wv, vec):
    f, s = idx[0], idx[1]
    refs = (a, b, c, d)
    for k, ref in enumerate(refs):
        columns = pl.ds(pl.multiple_of((s ^ k) * 128, 128), 128)
        for i, to in enumerate((wq, wk, wv)):
            to[:, columns] = ref[:64, i * 128 : (i + 1) * 128].astype(F32)
    tails = [ref[64:80, :].astype(F32) for ref in refs]
    summed = (tails[0] + tails[2]) + (tails[1] + tails[3])
    bias = jnp.zeros((1, 384), F32)
    for k in range(4):
        bias = bias + jnp.where((s ^ k) == f // 2, tails[k][0:1], 0.0)
    odd = (f & 1) == 1
    query, value = bias[:, :128], bias[:, 256:384]
    query = jnp.where(odd, half_roll(query), query)
    value = jnp.where(odd, half_roll(value), value)
    vec[0:1, 0:128] = query
    vec[1:2, 0:128] = value
    vec[0:1, 128:384] = summed[1:2, 128:384]
    vec[1:2, 128:256] = summed[2:3, 0:128]
    vec[1:2, 256:384] = jnp.zeros((1, 128), F32)
    vec[2:3, 0:256] = summed[2:3, 128:384]


def dx_core_kernel(idx, keep, got, stay, go):
    stay[...] = keep[0].astype(F32) + got[0].astype(F32)
    go[...] = (keep[1].astype(F32) + got[1].astype(F32)).astype(BF)


def dx_end_kernel(idx, e1, stay, got, out):
    out[...] = e1[...] + stay[...] + got[...].astype(F32)


def swap(values, axis, step):
    size = lax.axis_size(axis)
    return lax.ppermute(values, axis, [(i, i ^ step) for i in range(size)])


def body(
    inputs,
    block_ids,
    query_weight,
    query_bias,
    key_weight,
    value_weight,
    value_bias,
    out_weight,
    out_bias,
    gain_one,
    shift_one,
    up_weight,
    up_bias,
    down_weight,
    down_bias,
    gain_two,
    shift_two,
    cotangent,
):
    owners = lax.axis_size("fsdp")
    direct = owners == PARTS
    seq = lax.axis_index("seq").astype(jnp.int32)
    fsdp = lax.axis_index("fsdp").astype(jnp.int32)
    zero = jnp.zeros((), jnp.int32)
    index = jnp.stack([fsdp, seq, seq & 1]) if direct else jnp.stack([zero, seq, zero])
    _, part, width = inputs.shape
    own = inputs.reshape(part, width)
    across = swap(own, "seq", 2)
    xs = [own, swap(own, "seq", 1), across, swap(across, "seq", 1)]
    total = part * lax.axis_size("seq")
    vectors = (query_bias, value_bias, out_bias, gain_one, shift_one, gain_two, shift_two, down_bias)

    if direct:
        vec = jnp.concatenate((*vectors, up_bias)).reshape(2, 384)
        vec = jnp.pad(vec, ((0, 14), (0, 0)))
        head_part, up_part, down_part = run(
            pack_kernel,
            [((80, 384), BF), ((32, 2560), BF), ((128, 512), BF)],
            index,
            (query_weight, key_weight, value_weight, out_weight, up_weight, down_weight, vec),
        )
        evens = [head_part] + [swap(head_part, "fsdp", k) for k in (2, 4, 6)]
        odds = [swap(e, "fsdp", 1) for e in evens]
        heads = [p for pair in zip(evens, odds) for p in pair]

        def gathered(piece):
            mine = [piece] + [swap(piece, "fsdp", k) for k in (2, 4, 6)]
            (even,) = run(stack_kernel, [((4, *piece.shape), BF)], index, mine)
            odd = swap(even, "fsdp", 1)
            return even, odd, swap(even, "seq", 1), swap(odd, "seq", 1)

        ups, downs = gathered(up_part), gathered(down_part)
    else:

        def full(values):
            return lax.all_gather(values, "fsdp", axis=0, tiled=True)

        vec = jnp.concatenate([full(v).reshape(PARTS, 64) for v in vectors] + [full(up_bias).reshape(PARTS, 256)], axis=1)
        vec = jnp.pad(vec.reshape(PARTS, 2, 384), ((0, 0), (0, 14), (0, 0)))
        cut = [
            lax.dynamic_slice_in_dim(full(w), seq * 128, 128, 1)
            for w in (query_weight, key_weight, value_weight)
        ]
        packed = jnp.concatenate([jnp.concatenate(cut, axis=1).reshape(PARTS, 64, 384), vec], axis=1)
        heads = [packed[k] for k in range(PARTS)]
        wide = jnp.concatenate([full(out_weight), full(up_weight)], axis=1).reshape(4, 2, 64, 2560)
        ups = [wide[:, k & 1, (k >> 1) * 32 : (k >> 1) * 32 + 32] for k in range(4)]
        tall = full(down_weight).reshape(4, 2, 256, 512)
        downs = [tall[:, k & 1, (k >> 1) * 128 : (k >> 1) * 128 + 128] for k in range(4)]

    piece = ((part, 128), BF)
    *ms, qa, ka, v, m_heads, rinv = run(
        attend_kernel,
        [piece] * 4
        + [((2, total, 128), BF)] * 2
        + [((total, 128), BF)] * 2
        + [((total, 128), F32)],
        index,
        (*xs, *heads, block_ids),
        scratch=(
            ((512, 384), BF),
            ((PARTS, 384), F32),
            ((PARTS, 384), F32),
            ((total, 128), BF),
            ((total, 128), BF),
        ),
    )
    ms = [ms[0]] + [swap(ms[k], "seq", k) for k in (1, 2, 3)]
    result, *rest = run(
        middle_kernel,
        [((part, width), BF)]
        + [piece] * 4
        + [
            ((part, width), F32),
            ((part, 2048), BF),
            ((part, width), BF),
            ((part, width), BF),
            ((part, 2048), BF),
            ((part, width), BF),
            ((part, width), BF),
            ((PARTS, 16, 384), BF),
        ],
        index,
        (own, *ms, cotangent.reshape(part, width), *heads, *ups, *downs),
        scratch=(
            ((512, 512), BF),
            ((512, 2048), BF),
            ((2048, 512), BF),
            ((PARTS, 384), F32),
            ((PARTS, 384), F32),
            ((part, 2048), F32),
            ((part, width), BF),
            ((PARTS, 384), F32),
            ((PARTS, 384), F32),
        ),
    )
    ems, (e1, u, eb, y, ez, m, ea, vg) = rest[:4], rest[4:]
    ems = [ems[0]] + [swap(ems[k], "seq", k) for k in (1, 2, 3)]
    down_keep, down_send = run(
        down_grad_kernel, [((PARTS, 128, 512), BF)] * 2, index, (u, eb)
    )
    up_keep, up_send = run(
        up_grad_kernel, [((PARTS, 32, 2560), BF)] * 2, index, (y, ez, m, ea)
    )
    dx_keep, dx_send, w_keep, w_send = run(
        attend_back_kernel,
        [((2, part, width), BF)] * 2 + [((PARTS // 2, 80, 384), BF)] * 2,
        index,
        (*ems, qa, ka, v, m_heads, rinv, *xs, *heads, vg),
        scratch=(
            ((512, 384), BF),
            ((total, 128), BF),
            ((2, total, 128), BF),
            ((2, total, 128), BF),
            ((2, total, 128), F32),
            ((total, 384), BF),
            ((512, 384), F32),
        ),
    )

    stay, go = run(
        dx_core_kernel,
        [((part, width), F32), ((part, width), BF)],
        index,
        (dx_keep, swap(dx_send, "seq", 1)),
    )
    (input_grad,) = run(
        dx_end_kernel, [((part, width), F32)], index, (e1, stay, swap(go, "seq", 2))
    )

    if direct:

        def scattered(stay, go):
            rows, columns = stay.shape[1:]
            got = swap(go, "fsdp", 1)
            outs = run(y_sum_kernel, [((rows, columns), BF)] * 4, index, (stay, got))
            got = [swap(outs[k >> 1], "fsdp", k) for k in (2, 4, 6)]
            (mine,) = run(z_sum_kernel, [((rows, columns), BF)], index, (outs[0], *got))
            return (mine, *(swap(mine, "seq", k) for k in (1, 2, 3)))

        def halved(keep, send):
            rows, columns = keep.shape[1:]
            return run(
                core_sum_kernel,
                [((PARTS // 2, rows, columns), BF)] * 2,
                index,
                (keep, swap(send, "seq", 1)),
            )

        (down_grad,) = run(
            end_down_kernel,
            [((256, 512), F32)],
            index,
            scattered(*halved(down_keep, down_send)),
        )
        out_grad, up_grad = run(
            end_up_kernel,
            [((64, 512), F32), ((64, 2048), F32)],
            index,
            scattered(*halved(up_keep, up_send)),
        )
        wq_grad, wk_grad, wv_grad, vec = run(
            end_heads_kernel,
            [((64, 512), F32)] * 3 + [((3, 384), F32)],
            index,
            scattered(w_keep, w_send),
        )
        flat = vec.reshape(-1)
        small = [flat[k * 64 : (k + 1) * 64] for k in range(16)]
        qb_grad, _, ob_grad, g1_grad, s1_grad, g2_grad, vb_grad, _, s2_grad, db_grad = small[:10]
        ub_grad = flat[768:1024]
    else:

        def summed(values):
            values = lax.psum_scatter(values, "fsdp", scatter_dimension=0, tiled=True)
            return lax.psum(values.astype(BF), "seq").astype(F32)

        both = jnp.concatenate([down_keep, down_send], axis=1).reshape(2048, 512)
        down_grad = summed(both.astype(F32))
        both = jnp.concatenate([up_keep, up_send], axis=1).reshape(512, 2560)
        both = summed(both.astype(F32))
        out_grad, up_grad = both[:, :512], both[:, 512:]
        both = jnp.stack([w_keep, w_send], axis=1).reshape(PARTS, 80, 384).astype(F32)
        made = lax.psum_scatter(both[:, :64].reshape(512, 384), "fsdp", scatter_dimension=0, tiled=True)
        made = lax.all_gather(made.astype(BF), "seq", axis=0).astype(F32)
        wq_grad, wk_grad, wv_grad = (
            jnp.concatenate([made[t, :, i * 128 : (i + 1) * 128] for t in range(4)], axis=1)
            for i in range(3)
        )
        biases = lax.all_gather(lax.psum(both[0, 64], "fsdp").astype(BF), "seq", axis=0).astype(F32)
        cut = width // owners

        def mine(values):
            return lax.dynamic_slice_in_dim(values, fsdp * cut, cut, 0)

        qb_grad, vb_grad = mine(biases[:, :128].reshape(-1)), mine(biases[:, 256:].reshape(-1))
        flat = both[:, 65:67].reshape(PARTS, 768)
        ob_grad, g1_grad, s1_grad, g2_grad, s2_grad, db_grad = (
            summed(flat[:, k * 64 : (k + 1) * 64].reshape(-1)) for k in range(2, 8)
        )
        ub_grad = summed(flat[:, 512:].reshape(-1))

    return (
        result.reshape(inputs.shape),
        input_grad.reshape(inputs.shape),
        wq_grad,
        qb_grad,
        wk_grad,
        wv_grad,
        vb_grad,
        out_grad,
        ob_grad,
        g1_grad,
        s1_grad,
        up_grad,
        ub_grad,
        down_grad,
        db_grad,
        g2_grad,
        s2_grad,
    )


def solution(mesh):
    tokens, matrix, vector = P("fsdp", "seq", None), P("fsdp", None), P("fsdp")
    in_specs = (
        tokens,
        matrix,
        matrix,
        vector,
        matrix,
        matrix,
        vector,
        matrix,
        vector,
        vector,
        vector,
        matrix,
        vector,
        matrix,
        vector,
        vector,
        vector,
        tokens,
    )
    out_specs = (
        tokens,
        tokens,
        matrix,
        vector,
        matrix,
        matrix,
        vector,
        matrix,
        vector,
        vector,
        vector,
        matrix,
        vector,
        matrix,
        vector,
        vector,
        vector,
    )
    return jax.shard_map(body, mesh=mesh, in_specs=in_specs, out_specs=out_specs, check_vma=False)
```

```python
import functools
import math

import jax
import jax.numpy as jnp
from jax import lax
from jax.experimental import pallas as pl
from jax.experimental.pallas import tpu as pltpu
from jax.sharding import PartitionSpec as P

HEADS = 8
BLOCKS = 8
PARTS = 8
NORM_EPS = 1e-05
MASKED = -1e30
GELU_ROOT = 0.7978845608028654
GELU_CUBIC = 0.044715
BF = jnp.bfloat16
F32 = jnp.float32
COSTS = {}
VMEM = pl.BlockSpec(memory_space=pltpu.VMEM)
SMEM = pl.BlockSpec(memory_space=pltpu.SMEM)


def dot_nn(left, right):
    return lax.dot_general(left, right, (((1,), (0,)), ((), ())), preferred_element_type=F32)


def dot_nt(left, right):
    return lax.dot_general(left, right, (((1,), (1,)), ((), ())), preferred_element_type=F32)


def dot_tn(left, right):
    return lax.dot_general(left, right, (((0,), (0,)), ((), ())), preferred_element_type=F32)


def run(kernel, outs, index, args, scratch=()):
    cost = COSTS.get(kernel, 1.7)
    outs = [jax.ShapeDtypeStruct(*o) for o in outs]
    return pl.pallas_call(
        kernel,
        out_shape=outs,
        in_specs=[SMEM] + [VMEM] * len(args),
        out_specs=[VMEM] * len(outs),
        scratch_shapes=[pltpu.VMEM(*s) for s in scratch],
        compiler_params=pltpu.CompilerParams(vmem_limit_bytes=56 * 1024 * 1024),
        cost_estimate=pl.CostEstimate(flops=int(cost * 1e9), bytes_accessed=int(cost * 3e6), transcendentals=0),
    )(index, *args)


def lanes_of(shape):
    return lax.broadcasted_iota(jnp.int32, shape, len(shape) - 1)


def rows_of(shape):
    return lax.broadcasted_iota(jnp.int32, shape, len(shape) - 2)


def half_roll(values):
    return pltpu.roll(values, 64, 1)


def pack_kernel(idx, wq, wk, wv, wo, up, down, *refs):
    vectors, first_out, down_out, tail = refs[:9], *refs[9:]
    s, c, x = idx[1], idx[2], idx[3]
    columns = pl.ds(pl.multiple_of(s * 128, 128), 128)
    for i, ref in enumerate((wq, wk, wv)):
        first_out[:64, i * 128 : (i + 1) * 128] = ref[:, columns]
    tail[...] = jnp.zeros_like(tail)
    for k, ref in enumerate(vectors[:8]):
        tail[k // 6 : k // 6 + 1, (k % 6) * 64 : (k % 6 + 1) * 64] = ref[...].astype(F32).reshape(1, 64)
    tail[1:2, 128:384] = vectors[8][...].astype(F32).reshape(1, 256)
    first_out[64:80, :384] = tail[...].astype(BF)
    rows = pl.ds(pl.multiple_of(c * 32 + x * 16, 16), 16)
    first_out[:16, 384:] = wo[rows, :]
    for j in range(4):
        first_out[(j + 1) * 16 : (j + 2) * 16, 384:] = up[rows, j * 512 : (j + 1) * 512]
    down_out[...] = down[pl.ds(pl.multiple_of(c * 128, 128), 128), :]


def load_vectors(idx, even, odd, first, second):
    for k in range(PARTS):
        rows = (odd if k & 1 else even)[k >> 1, 64:80, :384].astype(F32)
        first[pl.ds(idx[0] ^ k, 1), :] = rows[0:1]
        second[pl.ds(idx[0] ^ k, 1), :] = rows[1:2]


def load_heads(idx, even, odd, weight):
    for k in range(PARTS):
        rows = pl.ds(pl.multiple_of((idx[0] ^ k) * 64, 64), 64)
        weight[rows, :] = (odd if k & 1 else even)[k >> 1, :64, :384]


def key_limit(i, part, count):
    return min((i + 2) * part, count * part)


def attend_kernel(idx, *refs):
    xs, even, odd, ids = refs[:4], *refs[4:7]
    ms = refs[7:11]
    qa, ka, v_out, m_out, rinv_out = refs[11:16]
    weight, first, second, q_s, k_s = refs[16:]
    s = idx[1]
    part = ms[0].shape[0]
    count = ids.shape[1] // part
    total = part * count
    load_heads(idx, even, odd, weight)
    load_vectors(idx, even, odd, first, second)
    left, right = first[pl.ds(2 * s, 1), :][:, :128], first[pl.ds(2 * s + 1, 1), :][:, :128]
    low_row = lanes_of((1, 128)) < 64
    query_bias = jnp.where(low_row, left, half_roll(right))
    value_bias = jnp.where(low_row, half_roll(left), right)
    for k, ref in enumerate(xs):
        rows = pl.ds(pl.multiple_of((s ^ k) * part, part), part)
        made = dot_nn(ref[-part:, :], weight[...])
        q_s[rows, :] = (made[:, :128] + query_bias).astype(BF)
        k_s[rows, :] = made[:, 128:256].astype(BF)
        v_out[rows, :] = (made[:, 256:] + value_bias).astype(BF)
    blocks = jnp.broadcast_to(ids[...], (128, total))
    row = rows_of((128, total))
    row = jnp.where(row >= 64, row - 64, row)
    own = jnp.where((row < BLOCKS) & (blocks == row), 1.0, 0.0).astype(F32).T
    barred = jnp.where(
        row < BLOCKS,
        jnp.where(blocks > row, MASKED, 0.0),
        jnp.where(row < BLOCKS + 3, 1.0, 0.0),
    ).astype(F32).T
    lane = lanes_of((total, 128))
    low = lane < 64
    queries = q_s[...].astype(F32) * (1.0 / math.sqrt(64))
    keys = k_s[...].astype(F32)
    qa[0] = jnp.where(low, queries, own).astype(BF)
    qa[1] = jnp.where(low, own, queries).astype(BF)
    ka[0] = jnp.where(low, keys, barred).astype(BF)
    ka[1] = jnp.where(low, barred, keys).astype(BF)
    lane = lanes_of((part, 128))
    low = lane < 64
    for i in range(count):
        rows = slice(i * part, (i + 1) * part)
        limit = key_limit(i, part, count)
        mixed = []
        sums = []
        for h in range(2):
            scores = dot_nt(qa[h, rows, :], ka[h, :limit, :])
            top = jnp.max(scores, axis=-1, keepdims=True)
            raised = jnp.exp(scores - top).astype(BF)
            values = v_out[:limit, :]
            mine = lanes_of(values.shape) < 64
            values = jnp.where(mine if h == 0 else ~mine, values, jnp.ones_like(values))
            made = dot_nn(raised, values)
            sums.append(1.0 / half_roll(made))
            mixed.append(made * sums[-1])
            high = top.astype(BF).astype(F32)
            middle = (top - high).astype(BF).astype(F32)
            rest = top - high - middle
            at = lane - (64 if h == 0 else 0) - BLOCKS
            tops = jnp.where(at == 0, -high, jnp.where(at == 1, -middle, jnp.where(at == 2, -rest, 0.0)))
            held = qa[h, rows, :].astype(F32)
            qa[h, rows, :] = jnp.where((at >= 0) & (at < 3), tops, held).astype(BF)
        m_out[rows, :] = jnp.where(low, mixed[0], mixed[1]).astype(BF)
        rinv_out[rows, :] = jnp.where(low, sums[0], sums[1])
    for k, ref in enumerate(ms):
        ref[...] = m_out[pl.ds(pl.multiple_of((s ^ k) * part, part), part), :]


def spread(block, upper, width):
    row = rows_of((PARTS, 128))
    match = (row & 1) == (1 if upper else 0)
    block = jnp.where(match, block, half_roll(block))
    tiled = jnp.concatenate([block] * (width // 128), axis=1)
    keep = lanes_of((PARTS, width)) // 64 == rows_of((PARTS, width))
    return jnp.sum(jnp.where(keep, tiled, 0.0), axis=0, keepdims=True)


def gather_up(vector, upper):
    width = vector.shape[1]
    keep = lanes_of((PARTS, width)) // 64 == rows_of((PARTS, width))
    picked = jnp.where(keep, jnp.broadcast_to(vector, (PARTS, width)), 0.0)
    block = sum(picked[:, j * 128 : (j + 1) * 128] for j in range(width // 128))
    match = (rows_of((PARTS, 128)) & 1) == (1 if upper else 0)
    return jnp.where(match, block, half_roll(block))


def normalize(summed):
    centre = summed - jnp.mean(summed, axis=-1, keepdims=True)
    inverse = lax.rsqrt(jnp.mean(centre * centre, axis=-1, keepdims=True) + NORM_EPS)
    return centre * inverse, inverse


def norm_back(grad, normed, inverse):
    first_mean = jnp.mean(grad, axis=-1, keepdims=True)
    cross_mean = jnp.mean(grad * normed, axis=-1, keepdims=True)
    return inverse * (grad - first_mean - normed * cross_mean)


def gelu(values):
    inner = GELU_ROOT * (values + GELU_CUBIC * values * values * values)
    return 0.5 * values * (1.0 + jnp.tanh(inner))


def gelu_slope(values):
    square = values * values
    inner = GELU_ROOT * (values + GELU_CUBIC * values * square)
    tanh_part = jnp.tanh(inner)
    return 0.5 * (1.0 + tanh_part) + 0.5 * values * (1.0 - tanh_part * tanh_part) * GELU_ROOT * (
        1.0 + 3.0 * GELU_CUBIC * square
    )


def column_sum(values):
    return jnp.sum(values.astype(F32), axis=0, keepdims=True)


def middle_kernel(idx, *refs):
    x0, ms, cot, even, odd = refs[0], refs[1:5], *refs[5:8]
    even_parts, odd_parts, down_parts = refs[8:11], refs[11:14], refs[14:18]
    out, ems, e1_out = refs[18], refs[19:23], refs[23]
    keep1, ship1, keep2, ship2, vg_out = refs[24:29]
    wo, up, down, first, second, z_s, em_s, m_s, u_s, ez_s, ea_s, rows0, rows1 = refs[29:]
    f, s, c, x = idx[0], idx[1], idx[2], idx[3]
    for k in range(4):
        row = (c ^ (k & 1)) * 32 + (x ^ (k >> 1)) * 16
        for slot in range(PARTS):
            j = slot >> 1
            if k == 0:
                block = (odd if slot & 1 else even)[j, :, 384:]
            elif slot & 1:
                block = odd_parts[k - 1][j]
            else:
                block = even_parts[k - 1][j * 80 : (j + 1) * 80, :]
            rows = pl.ds(pl.multiple_of((f ^ slot) * 64 + row, 16), 16)
            wo[rows, :] = block[:16]
            for i in range(4):
                up[rows, i * 512 : (i + 1) * 512] = block[(i + 1) * 16 : (i + 2) * 16]
    for which in range(4):
        half = c if which < 2 else 1 - c
        for j in range(4):
            owner = f ^ (2 * j + (which & 1))
            rows = pl.ds(pl.multiple_of(owner * 256 + half * 128, 128), 128)
            down[rows, :] = down_parts[which][j]
    load_vectors(idx, even, odd, first, second)
    v0, v1 = first[...], second[...]
    out_bias = spread(v0[:, 128:256], False, 512)
    gain_one = spread(v0[:, 128:256], True, 512)
    shift_one = spread(v0[:, 256:384], False, 512)
    gain_two = spread(v0[:, 256:384], True, 512)
    shift_two = spread(v1[:, 0:128], False, 512)
    down_bias = spread(v1[:, 0:128], True, 512)
    keep = lanes_of((PARTS, 2048)) // 256 == rows_of((PARTS, 2048))
    tiled = jnp.concatenate([v1[:, 128:384]] * 8, axis=1)
    up_bias = jnp.sum(jnp.where(keep, tiled, 0.0), axis=0, keepdims=True)

    for k, ref in enumerate(ms):
        m_s[:, pl.ds(pl.multiple_of((s ^ k) * 128, 128), 128)] = ref[...]
    h1 = x0[...].astype(F32) + (dot_nn(m_s[...], wo[...]) + out_bias)
    n1, r1 = normalize(h1)
    y = (n1 * gain_one + shift_one).astype(BF)
    branch = jnp.zeros(h1.shape, F32)
    for j in range(4):
        columns = slice(j * 512, (j + 1) * 512)
        z = dot_nn(y, up[:, columns]) + up_bias[:, columns]
        z_s[:, columns] = z
        u = gelu(z).astype(BF)
        for one in range(2):
            owner = 2 * j + one
            for half in range(2):
                at = one * 256 + half * 128
                u_s[half, :, owner * 128 : (owner + 1) * 128] = u[:, at : at + 128]
        branch = branch + dot_nn(u, down[columns, :])
    n2, r2 = normalize(y.astype(F32) + (branch + down_bias))
    out[...] = (n2 * gain_two + shift_two).astype(BF)
    grad = cot[...].astype(F32)
    gain_two_grad = column_sum(grad * n2)
    shift_two_grad = column_sum(grad)
    e2 = norm_back(grad * gain_two, n2, r2)
    eb = e2.astype(BF)
    down_bias_grad = column_sum(eb)
    ey = e2
    up_bias_grads = []
    for j in range(4):
        columns = slice(j * 512, (j + 1) * 512)
        eu = dot_nt(eb, down[columns, :]).astype(BF).astype(F32)
        ez = (eu * gelu_slope(z_s[:, columns])).astype(BF)
        ez_s[j // 2, :, (j % 2) * 512 : (j % 2 + 1) * 512] = ez
        up_bias_grads.append(column_sum(ez))
        ey = ey + dot_nt(ez, up[:, columns])
    gain_one_grad = column_sum(ey * n1)
    shift_one_grad = column_sum(ey)
    e1 = norm_back(ey * gain_one, n1, r1)
    e1_out[...] = e1
    ea = e1.astype(BF)
    ea_s[0], ea_s[1] = ea[:, :256], ea[:, 256:]
    out_bias_grad = column_sum(ea)
    em_s[...] = dot_nt(ea, wo[...]).astype(BF)
    for k, ref in enumerate(ems):
        ref[...] = em_s[:, pl.ds(pl.multiple_of((s ^ k) * 128, 128), 128)]
    for to1, to2, half in ((keep1, keep2, c), (ship1, ship2, 1 - c)):
        to1[:, :1024] = u_s[half]
        to1[:, 1024:] = eb
        to2[:, :1024] = ez_s[half]
        to2[:, 1024:1280] = ea_s[half]
        to2[:, 1280:1792] = y
        to2[:, 1792:] = m_s[...]
    rows0[:, :128] = jnp.zeros((PARTS, 128), F32)
    rows0[:, 128:256] = gather_up(out_bias_grad, False) + gather_up(gain_one_grad, True)
    rows0[:, 256:384] = gather_up(shift_one_grad, False) + gather_up(gain_two_grad, True)
    rows1[:, :128] = gather_up(shift_two_grad, False) + gather_up(down_bias_grad, True)
    up_bias_grad = jnp.concatenate(up_bias_grads, axis=1)
    picked = jnp.where(keep, jnp.broadcast_to(up_bias_grad, (PARTS, 2048)), 0.0)
    rows1[:, 128:384] = sum(picked[:, j * 256 : (j + 1) * 256] for j in range(8))
    at = rows_of((16, 384))
    for k in range(PARTS):
        a, b = rows0[k : k + 1, :], rows1[k : k + 1, :]
        vg_out[k] = jnp.where(at == 1, a, jnp.where(at == 2, b, 0.0)).astype(BF)


def down_grad_kernel(idx, mine, other, even, odd, send):
    f, x = idx[0], idx[3]
    for pair in range(PARTS // 2):
        columns = slice(pair * 256, (pair + 1) * 256)
        made = dot_tn(mine[:, columns], mine[:, 1024:]) + dot_tn(other[:, columns], other[:, 1024:])
        made = made.astype(BF)
        for one in range(2):
            slot = f ^ (2 * pair + one)
            upper, lower = made[one * 128 : one * 128 + 64], made[one * 128 + 64 : one * 128 + 128]
            kept, gone = jnp.where(x == 0, upper, lower), jnp.where(x == 0, lower, upper)
            odd_slot = slot & 1
            send[odd_slot * 4 + (slot >> 1)] = gone

            @pl.when(odd_slot == 0)
            def _():
                even[slot >> 1] = kept

            @pl.when(odd_slot == 1)
            def _():
                odd[slot >> 1] = kept


def up_grad_kernel(idx, mine, other, even, odd):
    f = idx[0]
    for pair in range(PARTS // 2):
        columns = slice(1280 + pair * 128, 1280 + (pair + 1) * 128)
        made_up = dot_tn(mine[:, columns], mine[:, :1024]) + dot_tn(other[:, columns], other[:, :1024])
        columns = slice(1792 + pair * 128, 1792 + (pair + 1) * 128)
        made_out = dot_tn(mine[:, columns], mine[:, 1024:1280]) + dot_tn(
            other[:, columns], other[:, 1024:1280]
        )
        for one in range(2):
            slot = f ^ (2 * pair + one)
            for parity, to in ((0, even), (1, odd)):

                @pl.when((slot & 1) == parity)
                def _():
                    to[slot >> 1, :, :1024] = made_up[one * 64 : (one + 1) * 64].astype(BF)
                    to[slot >> 1, :, 1024:] = made_out[one * 64 : (one + 1) * 64].astype(BF)


def attend_back_kernel(idx, *refs):
    ems, qa, ka, v, m, rinv = refs[:4], refs[4], refs[5], refs[6], refs[7], refs[8]
    xs, even, odd, vg = refs[9:13], *refs[13:16]
    dx_keep, dx_send, w_out = refs[16:19]
    weight, em_s, ema, va, eq_s, e_s = refs[19:]
    f, s = idx[0], idx[1]
    part = ems[0].shape[0]
    total = v.shape[0]
    count = total // part
    load_heads(idx, even, odd, weight)
    for k, ref in enumerate(ems):
        em_s[pl.ds(pl.multiple_of((s ^ k) * part, part), part), :] = ref[...]
    lane = lanes_of((total, 128))
    low = lane < 64
    inverse = rinv[...]
    em = em_s[...].astype(F32)
    scaled = em * inverse
    product = scaled * m[...].astype(F32)
    values = v[...]
    for h in range(2):
        mine = low if h == 0 else ~low
        delta = jnp.sum(jnp.where(mine, product, 0.0), axis=-1, keepdims=True)
        high = delta.astype(BF).astype(F32)
        at = lane - (64 if h == 0 else 0)
        extra = jnp.where(at == 0, -high, jnp.where(at == 1, high - delta, 0.0))
        ema[h] = jnp.where(mine, scaled, extra).astype(BF)
        ones = jnp.where((at == 0) | (at == 1), 1.0, 0.0)
        va[h] = jnp.where(mine, values.astype(F32), ones).astype(BF)
    lane = lanes_of((part, 128))
    low = lane < 64
    eq_s[...] = jnp.zeros_like(eq_s)
    for j in range(count):
        rows = slice(j * part, (j + 1) * part)
        start = max(j - 1, 0) * part
        grad_keys, grad_values = [], []
        for h in range(2):
            raised = jnp.exp(dot_nt(ka[h, rows, :], qa[h, start:, :]))
            slopes = dot_nt(va[h, rows, :], ema[h, start:, :])
            grad = (raised * slopes).astype(BF)
            grad_keys.append(dot_nn(grad, qa[h, start:, :]))
            grad_values.append(dot_nn(raised.astype(BF), ema[h, start:, :]))
            eq_s[h, start:, :] += dot_tn(grad, ka[h, rows, :])
        e_s[rows, 128:256] = jnp.where(low, grad_keys[0], grad_keys[1]).astype(BF)
        e_s[rows, 256:384] = jnp.where(low, grad_values[0], grad_values[1]).astype(BF)
    lane = lanes_of((total, 128))
    e_s[:, :128] = (jnp.where(lane < 64, eq_s[0], eq_s[1]) * (1.0 / math.sqrt(64))).astype(BF)
    wg = jnp.zeros(weight.shape, F32)
    for k in range(4):
        grads = e_s[pl.ds(pl.multiple_of((s ^ k) * part, part), part), :]
        wg = wg + dot_tn(xs[k][-part:, :], grads)
        made = dot_nt(grads, weight[...]).astype(BF)
        if k & 1:
            dx_send[k >> 1] = made
        else:
            dx_keep[k >> 1] = made
    bias = column_sum(e_s[...])
    at = rows_of((16, 384))
    middle = (lanes_of((16, 384)) >= 128) & (lanes_of((16, 384)) < 256)
    bias = jnp.where((at == 0) & ~middle, jnp.broadcast_to(bias, (16, 384)), 0.0)
    for k in range(PARTS):
        w_out[k, :64, :] = wg[k * 64 : (k + 1) * 64].astype(BF)
        w_out[k, 64:80, :] = (vg[k].astype(F32) + bias).astype(BF)


def plus(*terms):
    return functools.reduce(jnp.add, [t.astype(F32) for t in terms]).astype(BF)


def end_wide_kernel(idx, a, b, c, d, out_grad, up_grad, down_grad):
    core, x = idx[2], idx[3]
    wide = slice(0, 1280)
    own = a[:, wide].astype(F32) + c[:, wide].astype(F32)
    other = b[:, wide].astype(F32) + d[:, wide].astype(F32)
    left, right = jnp.where(core == 0, own, other), jnp.where(core == 0, other, own)
    up_grad[:, :1024], up_grad[:, 1024:] = left[:, :1024], right[:, :1024]
    out_grad[:, :256], out_grad[:, 256:] = left[:, 1024:], right[:, 1024:]
    for k, ref in enumerate((a, b, c, d)):
        at = (core ^ (k & 1)) * 128 + (x ^ (k >> 1)) * 64
        down_grad[pl.ds(pl.multiple_of(at, 64), 64), :] = ref[:, 1280:].astype(F32)


def end_heads_kernel(idx, a, b, c, d, wq, wk, wv, qb, vb, ob, g1, s1, g2, s2, db, ub):
    f, s = idx[0], idx[1]
    refs = (a, b, c, d)
    for k, ref in enumerate(refs):
        columns = pl.ds(pl.multiple_of((s ^ k) * 128, 128), 128)
        for i, to in enumerate((wq, wk, wv)):
            to[:, columns] = ref[:64, i * 128 : (i + 1) * 128].astype(F32)
    tails = [ref[64:80, :].astype(F32) for ref in refs]
    summed = (tails[0] + tails[2]) + (tails[1] + tails[3])
    bias = jnp.zeros((1, 384), F32)
    for k in range(4):
        bias = bias + jnp.where((s ^ k) == f // 2, tails[k][0:1], 0.0)
    odd = (f & 1) == 1
    for to, row in ((qb, bias[:, :128]), (vb, bias[:, 256:384])):
        to[...] = jnp.where(odd, half_roll(row), row)[:, :64].reshape(64)
    for k, to in enumerate((ob, g1, s1, g2, s2, db)):
        row, at = (summed[1:2], k + 2) if k < 4 else (summed[2:3], k - 4)
        to[...] = row[:, at * 64 : (at + 1) * 64].reshape(64)
    ub[...] = summed[2:3, 128:384].reshape(256)


COSTS.update(
    {
        attend_kernel: 0.5,
        middle_kernel: 10.2,
        down_grad_kernel: 3.4,
        up_grad_kernel: 4.0,
        attend_back_kernel: 9.3,
    }
)


def after(values, *others):
    return lax.optimization_barrier((values, *others))[0]


def swap(values, axis, step):
    size = lax.axis_size(axis)
    return lax.ppermute(values, axis, [(i, i ^ step) for i in range(size)])


def body(
    inputs,
    block_ids,
    query_weight,
    query_bias,
    key_weight,
    value_weight,
    value_bias,
    out_weight,
    out_bias,
    gain_one,
    shift_one,
    up_weight,
    up_bias,
    down_weight,
    down_bias,
    gain_two,
    shift_two,
    cotangent,
):
    owners = lax.axis_size("fsdp")
    direct = owners == PARTS
    seq = lax.axis_index("seq").astype(jnp.int32)
    fsdp = lax.axis_index("fsdp").astype(jnp.int32)
    zero = jnp.zeros((), jnp.int32)
    index = jnp.stack([fsdp if direct else zero, seq, seq & 1, seq >> 1])
    _, part, width = inputs.shape
    own = inputs.reshape(part, width)
    total = part * lax.axis_size("seq")
    vectors = (query_bias, value_bias, out_bias, gain_one, shift_one, gain_two, shift_two, down_bias)

    if direct:
        first_part, down_part = run(
            pack_kernel,
            [((80, 896), BF), ((128, 512), BF)],
            index,
            (
                query_weight,
                key_weight,
                value_weight,
                out_weight,
                up_weight,
                down_weight,
                *vectors,
                up_bias,
            ),
            scratch=(((16, 384), F32),),
        )
        def along_z(piece):
            return [piece] + [swap(piece, "fsdp", k) for k in (2, 4, 6)]

        mine = along_z(first_part)
        down_part = after(down_part, mine[1])
        even = jnp.stack(mine)
        odd = swap(even, "fsdp", 1)
        shared = jnp.concatenate([even[:, :, 384:].reshape(320, 512), own])
        across = swap(shared, "seq", 2)
        evens = [swap(shared, "seq", 1), across, swap(across, "seq", 1)]
        xs = [own, *evens]
        down_even = jnp.stack(along_z(down_part))
        down_odd = swap(down_even, "fsdp", 1)
        odd_wide = odd[:, :, 384:]
        odd_across = swap(odd_wide, "seq", 2)
        odds = [swap(odd_wide, "seq", 1), odd_across]
    else:

        def full(values):
            return lax.all_gather(values, "fsdp", axis=0, tiled=True)

        vec = jnp.concatenate([full(v).reshape(PARTS, 64) for v in vectors] + [full(up_bias).reshape(PARTS, 256)], axis=1)
        vec = jnp.pad(vec.reshape(PARTS, 2, 384), ((0, 0), (0, 14), (0, 0)))
        cut = [
            lax.dynamic_slice_in_dim(full(w), seq * 128, 128, 1)
            for w in (query_weight, key_weight, value_weight)
        ]
        across = swap(own, "seq", 2)
        xs = [own, swap(own, "seq", 1), across, swap(across, "seq", 1)]
        heads = jnp.concatenate([jnp.concatenate(cut, axis=1).reshape(PARTS, 64, 384), vec], axis=1)
        core, x = seq & 1, seq >> 1
        wide = jnp.concatenate([full(out_weight), full(up_weight)], axis=1).reshape(PARTS, 64, 5, 512)
        blocks = []
        for k in range(4):
            at = (core ^ (k & 1)) * 32 + (x ^ (k >> 1)) * 16
            block = lax.dynamic_slice_in_dim(wide, at, 16, 1)
            blocks.append(block.transpose(0, 2, 1, 3).reshape(4, 2, 80, 512))
        both = jnp.concatenate([heads.reshape(4, 2, 80, 384), blocks[0]], axis=-1)
        even, odd = both[:, 0], both[:, 1]
        evens = [b[:, 0].reshape(320, 512) for b in blocks[1:]]
        odds = [b[:, 1] for b in blocks[1:]]
        tall = full(down_weight).reshape(4, 2, 256, 512)
        downs = []
        for k in range(4):
            downs.append(lax.dynamic_slice_in_dim(tall[:, k & 1], (core ^ (k >> 1)) * 128, 128, 1))

    piece = ((part, 128), BF)
    *ms, qa, ka, v, m_heads, rinv = run(
        attend_kernel,
        [piece] * 4
        + [((2, total, 128), BF)] * 2
        + [((total, 128), BF)] * 2
        + [((total, 128), F32)],
        index,
        (*xs, even, odd, block_ids),
        scratch=(
            ((512, 384), BF),
            ((PARTS, 384), F32),
            ((PARTS, 384), F32),
            ((total, 128), BF),
            ((total, 128), BF),
        ),
    )
    if direct:
        odds.append(swap(after(odd_across, ms[0]), "seq", 1))
        downs = [down_even, down_odd, swap(down_even, "seq", 1)]
        downs.append(swap(after(down_odd, ms[0]), "seq", 1))
    ms = [ms[0]] + [swap(ms[k], "seq", k) for k in (1, 2, 3)]
    result, *rest = run(
        middle_kernel,
        [((part, width), BF)]
        + [piece] * 4
        + [((part, width), F32)]
        + [((part, 1536), BF)] * 2
        + [((part, 2304), BF)] * 2
        + [((PARTS, 16, 384), BF)],
        index,
        (own, *ms, cotangent.reshape(part, width), even, odd, *evens, *odds, *downs),
        scratch=(
            ((512, 512), BF),
            ((512, 2048), BF),
            ((2048, 512), BF),
            ((PARTS, 384), F32),
            ((PARTS, 384), F32),
            ((part, 2048), F32),
            ((part, width), BF),
            ((part, width), BF),
            ((2, part, 1024), BF),
            ((2, part, 1024), BF),
            ((2, part, 256), BF),
            ((PARTS, 384), F32),
            ((PARTS, 384), F32),
        ),
    )
    ems, (e1, keep1, ship1, keep2, ship2, vg) = rest[:4], rest[4:]
    ems = [ems[0]] + [swap(ems[k], "seq", k) for k in (1, 2, 3)]
    up_even_grad, up_odd_grad = run(
        up_grad_kernel, [((4, 64, 1280), BF)] * 2, index, (keep2, swap(ship2, "seq", 1))
    )
    down_even, down_odd, down_send = run(
        down_grad_kernel,
        [((4, 64, 512), BF)] * 2 + [((8, 64, 512), BF)],
        index,
        (after(keep1, up_even_grad), swap(ship1, "seq", 1)),
    )
    dx_keep, dx_send, w_grad = run(
        attend_back_kernel,
        [((2, part, width), BF)] * 2 + [((PARTS, 80, 384), BF)],
        index,
        (*ems, after(qa, down_even), ka, v, m_heads, rinv, *xs, even, odd, vg),
        scratch=(
            ((512, 384), BF),
            ((total, 128), BF),
            ((2, total, 128), BF),
            ((2, total, 128), BF),
            ((2, total, 128), F32),
            ((total, 384), BF),
        ),
    )

    down_got = swap(down_send, "seq", 2)
    dx_send, down_got = lax.optimization_barrier((dx_send, down_got))
    got = swap(dx_send, "seq", 1)
    if direct:
        up_got = swap(up_odd_grad, "fsdp", 1)
        dx_keep, up_got = lax.optimization_barrier((dx_keep, up_got))
    far = swap(plus(dx_keep[1], got[1]), "seq", 2)
    input_grad = e1 + ((dx_keep[0].astype(F32) + got[0].astype(F32)) + far.astype(F32))

    if direct:

        def spread_out(mine):
            return (mine, *(swap(mine, "seq", k) for k in (1, 2, 3)))

        def cross(values):
            return [swap(values[k >> 1], "fsdp", k) for k in (2, 4, 6)]

        up_sums = [plus(up_even_grad[k], up_got[k]) for k in range(4)]
        down_got = after(down_got, dx_send)
        down_far = swap(plus(down_odd, down_got[4:]), "fsdp", 1)
        down_stay = plus(down_even, down_got[:4])
        down_far = after(down_far, *up_sums, far)
        down_sums = [plus(down_stay[k], down_far[k]) for k in range(4)]
        sums = [jnp.concatenate(pair, axis=1) for pair in zip(up_sums, down_sums)]
        sums_far = cross(sums)
        w_made = after(lax.all_to_all(w_grad, "fsdp", 0, 0, tiled=True), *down_sums)
        w_made = jnp.sum(w_made.astype(F32), axis=0).astype(BF)
        w_all = spread_out(w_made)
        all_sums = spread_out(plus(sums[0], *after(tuple(sums_far), w_made)))
        (
            wq_grad,
            wk_grad,
            wv_grad,
            qb_grad,
            vb_grad,
            ob_grad,
            g1_grad,
            s1_grad,
            g2_grad,
            s2_grad,
            db_grad,
            ub_grad,
        ) = run(
            end_heads_kernel,
            [((64, 512), F32)] * 3 + [((64,), F32)] * 8 + [((256,), F32)],
            index,
            w_all,
        )
        out_grad, up_grad, down_grad = run(
            end_wide_kernel,
            [((64, 512), F32), ((64, 2048), F32), ((256, 512), F32)],
            index,
            all_sums,
        )
    else:

        def summed(values):
            values = lax.psum_scatter(values, "fsdp", scatter_dimension=0, tiled=True)
            return lax.psum(values.astype(BF), "seq").astype(F32)

        kept = [plus(down_even, down_got[:4]), plus(down_odd, down_got[4:])]
        kept = lax.all_gather(jnp.stack(kept, axis=1).reshape(PARTS, 64, 512), "seq", axis=0)
        kept = kept.reshape(2, 2, PARTS, 64, 512).transpose(2, 1, 0, 3, 4).reshape(2048, 512)
        down_grad = lax.psum_scatter(kept.astype(F32), "fsdp", scatter_dimension=0, tiled=True)
        kept = lax.all_gather(jnp.stack([up_even_grad, up_odd_grad], axis=1).reshape(512, 1280), "seq", axis=0)
        kept = kept.astype(F32).reshape(2, 2, 512, 1280)
        kept = lax.psum_scatter(kept[0] + kept[1], "fsdp", scatter_dimension=1, tiled=True)
        up_grad = jnp.concatenate([kept[0, :, :1024], kept[1, :, :1024]], axis=1)
        out_grad = jnp.concatenate([kept[0, :, 1024:], kept[1, :, 1024:]], axis=1)
        both = w_grad.astype(F32)
        made = lax.psum_scatter(both[:, :64].reshape(512, 384), "fsdp", scatter_dimension=0, tiled=True)
        made = lax.all_gather(made.astype(BF), "seq", axis=0).astype(F32)
        wq_grad, wk_grad, wv_grad = (
            jnp.concatenate([made[t, :, i * 128 : (i + 1) * 128] for t in range(4)], axis=1)
            for i in range(3)
        )
        biases = lax.all_gather(lax.psum(both[0, 64], "fsdp").astype(BF), "seq", axis=0).astype(F32)
        cut = width // owners

        def mine(values):
            return lax.dynamic_slice_in_dim(values, fsdp * cut, cut, 0)

        qb_grad, vb_grad = mine(biases[:, :128].reshape(-1)), mine(biases[:, 256:].reshape(-1))
        flat = both[:, 65:67].reshape(PARTS, 768)
        ob_grad, g1_grad, s1_grad, g2_grad, s2_grad, db_grad = (
            summed(flat[:, k * 64 : (k + 1) * 64].reshape(-1)) for k in range(2, 8)
        )
        ub_grad = summed(flat[:, 512:].reshape(-1))

    return (
        result.reshape(inputs.shape),
        input_grad.reshape(inputs.shape),
        wq_grad,
        qb_grad,
        wk_grad,
        wv_grad,
        vb_grad,
        out_grad,
        ob_grad,
        g1_grad,
        s1_grad,
        up_grad,
        ub_grad,
        down_grad,
        db_grad,
        g2_grad,
        s2_grad,
    )


def solution(mesh):
    tokens, matrix, vector = P("fsdp", "seq", None), P("fsdp", None), P("fsdp")
    in_specs = (
        tokens,
        matrix,
        matrix,
        vector,
        matrix,
        matrix,
        vector,
        matrix,
        vector,
        vector,
        vector,
        matrix,
        vector,
        matrix,
        vector,
        vector,
        vector,
        tokens,
    )
    out_specs = (
        tokens,
        tokens,
        matrix,
        vector,
        matrix,
        matrix,
        vector,
        matrix,
        vector,
        vector,
        vector,
        matrix,
        vector,
        matrix,
        vector,
        vector,
        vector,
    )
    return jax.shard_map(body, mesh=mesh, in_specs=in_specs, out_specs=out_specs, check_vma=False)
```

```python
import functools
import math

import jax
import jax.numpy as jnp
from jax import lax
from jax.experimental import pallas as pl
from jax.experimental.pallas import tpu as pltpu
from jax.sharding import PartitionSpec as P

HEADS = 8
BLOCKS = 8
PARTS = 8
NORM_EPS = 1e-05
MASKED = -1e30
GELU_ROOT = 0.7978845608028654
GELU_CUBIC = 0.044715
BF = jnp.bfloat16
F32 = jnp.float32
COSTS = {}
VMEM = pl.BlockSpec(memory_space=pltpu.VMEM)
SMEM = pl.BlockSpec(memory_space=pltpu.SMEM)


def dot_nn(left, right):
    return lax.dot_general(left, right, (((1,), (0,)), ((), ())), preferred_element_type=F32)


def dot_nt(left, right):
    return lax.dot_general(left, right, (((1,), (1,)), ((), ())), preferred_element_type=F32)


def dot_tn(left, right):
    return lax.dot_general(left, right, (((0,), (0,)), ((), ())), preferred_element_type=F32)


def run(kernel, outs, index, args, scratch=(), room=20):
    cost = COSTS.get(kernel, 1.7)
    outs = [jax.ShapeDtypeStruct(*o) for o in outs]
    return pl.pallas_call(
        kernel,
        out_shape=outs,
        in_specs=[SMEM] + [VMEM] * len(args),
        out_specs=[VMEM] * len(outs),
        scratch_shapes=[pltpu.VMEM(*s) for s in scratch],
        compiler_params=pltpu.CompilerParams(vmem_limit_bytes=room * 1024 * 1024),
        cost_estimate=pl.CostEstimate(flops=int(cost * 1e9), bytes_accessed=int(cost * 3e6), transcendentals=0),
    )(index, *args)


def lanes_of(shape):
    return lax.broadcasted_iota(jnp.int32, shape, len(shape) - 1)


def rows_of(shape):
    return lax.broadcasted_iota(jnp.int32, shape, len(shape) - 2)


def half_roll(values):
    return pltpu.roll(values, 64, 1)


def pack_kernel(idx, wq, wk, wv, wo, up, down, *refs):
    vectors, first_out, down_out, tail = refs[:9], *refs[9:]
    s, c, x = idx[1], idx[2], idx[3]
    columns = pl.ds(pl.multiple_of(s * 128, 128), 128)
    for i, ref in enumerate((wq, wk, wv)):
        first_out[:64, i * 128 : (i + 1) * 128] = ref[:, columns]
    tail[...] = jnp.zeros_like(tail)
    for k, ref in enumerate(vectors[:8]):
        tail[k // 6 : k // 6 + 1, (k % 6) * 64 : (k % 6 + 1) * 64] = ref[...].astype(F32).reshape(1, 64)
    tail[1:2, 128:384] = vectors[8][...].astype(F32).reshape(1, 256)
    first_out[64:80, :384] = tail[...].astype(BF)
    rows = pl.ds(pl.multiple_of(c * 32 + x * 16, 16), 16)
    first_out[:16, 384:] = wo[rows, :]
    for j in range(4):
        first_out[(j + 1) * 16 : (j + 2) * 16, 384:] = up[rows, j * 512 : (j + 1) * 512]
    down_out[...] = down[pl.ds(pl.multiple_of(c * 128, 128), 128), :]


def load_vectors(idx, even, odd, first, second):
    for k in range(PARTS):
        rows = (odd if k & 1 else even)[k >> 1, 64:80, :384].astype(F32)
        first[pl.ds(idx[0] ^ k, 1), :] = rows[0:1]
        second[pl.ds(idx[0] ^ k, 1), :] = rows[1:2]


def load_heads(idx, even, odd, weight):
    for k in range(PARTS):
        rows = pl.ds(pl.multiple_of((idx[0] ^ k) * 64, 64), 64)
        weight[rows, :] = (odd if k & 1 else even)[k >> 1, :64, :384]


def key_limit(i, part, count):
    return min((i + 2) * part, count * part)


def attend_kernel(idx, *refs):
    xs, even, odd, ids = refs[:4], *refs[4:7]
    ms = refs[7:11]
    qa, ka, v_out, m_out, rinv_out = refs[11:16]
    weight, first, second, q_s, k_s = refs[16:]
    s = idx[1]
    part = ms[0].shape[0]
    count = ids.shape[1] // part
    total = part * count
    load_heads(idx, even, odd, weight)
    load_vectors(idx, even, odd, first, second)
    left, right = first[pl.ds(2 * s, 1), :][:, :128], first[pl.ds(2 * s + 1, 1), :][:, :128]
    low_row = lanes_of((1, 128)) < 64
    query_bias = jnp.where(low_row, left, half_roll(right))
    value_bias = jnp.where(low_row, half_roll(left), right)
    for k, ref in enumerate(xs):
        rows = pl.ds(pl.multiple_of((s ^ k) * part, part), part)
        made = dot_nn(ref[-part:, :], weight[...])
        q_s[rows, :] = (made[:, :128] + query_bias).astype(BF)
        k_s[rows, :] = made[:, 128:256].astype(BF)
        v_out[rows, :] = (made[:, 256:] + value_bias).astype(BF)
    blocks = jnp.broadcast_to(ids[...], (128, total))
    row = rows_of((128, total))
    row = jnp.where(row >= 64, row - 64, row)
    own = jnp.where((row < BLOCKS) & (blocks == row), 1.0, 0.0).astype(F32).T
    barred = jnp.where(
        row < BLOCKS,
        jnp.where(blocks > row, MASKED, 0.0),
        jnp.where(row < BLOCKS + 3, 1.0, 0.0),
    ).astype(F32).T
    lane = lanes_of((total, 128))
    low = lane < 64
    queries = q_s[...].astype(F32) * (1.0 / math.sqrt(64))
    keys = k_s[...].astype(F32)
    qa[0] = jnp.where(low, queries, own).astype(BF)
    qa[1] = jnp.where(low, own, queries).astype(BF)
    ka[0] = jnp.where(low, keys, barred).astype(BF)
    ka[1] = jnp.where(low, barred, keys).astype(BF)
    lane = lanes_of((part, 128))
    low = lane < 64
    for i in range(count):
        rows = slice(i * part, (i + 1) * part)
        limit = key_limit(i, part, count)
        mixed = []
        sums = []
        for h in range(2):
            scores = dot_nt(qa[h, rows, :], ka[h, :limit, :])
            top = jnp.max(scores, axis=-1, keepdims=True)
            raised = jnp.exp(scores - top).astype(BF)
            values = v_out[:limit, :]
            mine = lanes_of(values.shape) < 64
            values = jnp.where(mine if h == 0 else ~mine, values, jnp.ones_like(values))
            made = dot_nn(raised, values)
            sums.append(1.0 / half_roll(made))
            mixed.append(made * sums[-1])
            high = top.astype(BF).astype(F32)
            middle = (top - high).astype(BF).astype(F32)
            rest = top - high - middle
            at = lane - (64 if h == 0 else 0) - BLOCKS
            tops = jnp.where(at == 0, -high, jnp.where(at == 1, -middle, jnp.where(at == 2, -rest, 0.0)))
            held = qa[h, rows, :].astype(F32)
            qa[h, rows, :] = jnp.where((at >= 0) & (at < 3), tops, held).astype(BF)
        m_out[rows, :] = jnp.where(low, mixed[0], mixed[1]).astype(BF)
        rinv_out[rows, :] = jnp.where(low, sums[0], sums[1])
    for k, ref in enumerate(ms):
        ref[...] = m_out[pl.ds(pl.multiple_of((s ^ k) * part, part), part), :]


def spread(block, upper, width):
    row = rows_of((PARTS, 128))
    match = (row & 1) == (1 if upper else 0)
    block = jnp.where(match, block, half_roll(block))
    tiled = jnp.concatenate([block] * (width // 128), axis=1)
    keep = lanes_of((PARTS, width)) // 64 == rows_of((PARTS, width))
    return jnp.sum(jnp.where(keep, tiled, 0.0), axis=0, keepdims=True)


def gather_up(vector, upper):
    width = vector.shape[1]
    keep = lanes_of((PARTS, width)) // 64 == rows_of((PARTS, width))
    picked = jnp.where(keep, jnp.broadcast_to(vector, (PARTS, width)), 0.0)
    block = sum(picked[:, j * 128 : (j + 1) * 128] for j in range(width // 128))
    match = (rows_of((PARTS, 128)) & 1) == (1 if upper else 0)
    return jnp.where(match, block, half_roll(block))


def normalize(summed):
    centre = summed - jnp.mean(summed, axis=-1, keepdims=True)
    inverse = lax.rsqrt(jnp.mean(centre * centre, axis=-1, keepdims=True) + NORM_EPS)
    return centre * inverse, inverse


def norm_back(grad, normed, inverse):
    first_mean = jnp.mean(grad, axis=-1, keepdims=True)
    cross_mean = jnp.mean(grad * normed, axis=-1, keepdims=True)
    return inverse * (grad - first_mean - normed * cross_mean)


def gelu(values):
    inner = GELU_ROOT * (values + GELU_CUBIC * values * values * values)
    return 0.5 * values * (1.0 + jnp.tanh(inner))


def gelu_slope(values):
    square = values * values
    inner = GELU_ROOT * (values + GELU_CUBIC * values * square)
    tanh_part = jnp.tanh(inner)
    return 0.5 * (1.0 + tanh_part) + 0.5 * values * (1.0 - tanh_part * tanh_part) * GELU_ROOT * (
        1.0 + 3.0 * GELU_CUBIC * square
    )


def column_sum(values):
    return jnp.sum(values.astype(F32), axis=0, keepdims=True)


def middle_kernel(idx, *refs):
    x0, ms, cot, even, odd = refs[0], refs[1:5], *refs[5:8]
    even_parts, odd_parts, down_parts = refs[8:11], refs[11:14], refs[14:18]
    out, ems, e1_out = refs[18], refs[19:23], refs[23]
    keep1, ship1, keep2, ship2, vg_out = refs[24:29]
    wo, up, down, first, second, z_s, em_s, m_s, u_s, ez_s, ea_s, rows0, rows1 = refs[29:]
    f, s, c, x = idx[0], idx[1], idx[2], idx[3]
    for k in range(4):
        row = (c ^ (k & 1)) * 32 + (x ^ (k >> 1)) * 16
        for slot in range(PARTS):
            j = slot >> 1
            if k == 0:
                block = (odd if slot & 1 else even)[j, :, 384:]
            elif slot & 1:
                block = odd_parts[k - 1][j]
            else:
                block = even_parts[k - 1][j * 80 : (j + 1) * 80, :]
            rows = pl.ds(pl.multiple_of((f ^ slot) * 64 + row, 16), 16)
            wo[rows, :] = block[:16]
            for i in range(4):
                up[rows, i * 512 : (i + 1) * 512] = block[(i + 1) * 16 : (i + 2) * 16]
    for which in range(4):
        half = c if which < 2 else 1 - c
        for j in range(4):
            owner = f ^ (2 * j + (which & 1))
            rows = pl.ds(pl.multiple_of(owner * 256 + half * 128, 128), 128)
            down[rows, :] = down_parts[which][j]
    load_vectors(idx, even, odd, first, second)
    v0, v1 = first[...], second[...]
    out_bias = spread(v0[:, 128:256], False, 512)
    gain_one = spread(v0[:, 128:256], True, 512)
    shift_one = spread(v0[:, 256:384], False, 512)
    gain_two = spread(v0[:, 256:384], True, 512)
    shift_two = spread(v1[:, 0:128], False, 512)
    down_bias = spread(v1[:, 0:128], True, 512)
    keep = lanes_of((PARTS, 2048)) // 256 == rows_of((PARTS, 2048))
    tiled = jnp.concatenate([v1[:, 128:384]] * 8, axis=1)
    up_bias = jnp.sum(jnp.where(keep, tiled, 0.0), axis=0, keepdims=True)

    for k, ref in enumerate(ms):
        m_s[:, pl.ds(pl.multiple_of((s ^ k) * 128, 128), 128)] = ref[...]
    h1 = x0[...].astype(F32) + (dot_nn(m_s[...], wo[...]) + out_bias)
    n1, r1 = normalize(h1)
    y = (n1 * gain_one + shift_one).astype(BF)
    branch = jnp.zeros(h1.shape, F32)
    for j in range(4):
        columns = slice(j * 512, (j + 1) * 512)
        z = dot_nn(y, up[:, columns]) + up_bias[:, columns]
        z_s[:, columns] = z
        u = gelu(z).astype(BF)
        for one in range(2):
            owner = 2 * j + one
            for half in range(2):
                at = one * 256 + half * 128
                u_s[half, :, owner * 128 : (owner + 1) * 128] = u[:, at : at + 128]
        branch = branch + dot_nn(u, down[columns, :])
    n2, r2 = normalize(y.astype(F32) + (branch + down_bias))
    out[...] = (n2 * gain_two + shift_two).astype(BF)
    grad = cot[...].astype(F32)
    gain_two_grad = column_sum(grad * n2)
    shift_two_grad = column_sum(grad)
    e2 = norm_back(grad * gain_two, n2, r2)
    eb = e2.astype(BF)
    down_bias_grad = column_sum(eb)
    ey = e2
    up_bias_grads = []
    for j in range(4):
        columns = slice(j * 512, (j + 1) * 512)
        eu = dot_nt(eb, down[columns, :]).astype(BF).astype(F32)
        ez = (eu * gelu_slope(z_s[:, columns])).astype(BF)
        ez_s[j // 2, :, (j % 2) * 512 : (j % 2 + 1) * 512] = ez
        up_bias_grads.append(column_sum(ez))
        ey = ey + dot_nt(ez, up[:, columns])
    gain_one_grad = column_sum(ey * n1)
    shift_one_grad = column_sum(ey)
    e1 = norm_back(ey * gain_one, n1, r1)
    e1_out[...] = e1
    ea = e1.astype(BF)
    ea_s[0], ea_s[1] = ea[:, :256], ea[:, 256:]
    out_bias_grad = column_sum(ea)
    em_s[...] = dot_nt(ea, wo[...]).astype(BF)
    for k, ref in enumerate(ems):
        ref[...] = em_s[:, pl.ds(pl.multiple_of((s ^ k) * 128, 128), 128)]
    for to1, to2, half in ((keep1, keep2, c), (ship1, ship2, 1 - c)):
        to1[:, :1024] = u_s[half]
        to1[:, 1024:] = eb
        to2[:, :1024] = ez_s[half]
        to2[:, 1024:1280] = ea_s[half]
        to2[:, 1280:1792] = y
        to2[:, 1792:] = m_s[...]
    rows0[:, :128] = jnp.zeros((PARTS, 128), F32)
    rows0[:, 128:256] = gather_up(out_bias_grad, False) + gather_up(gain_one_grad, True)
    rows0[:, 256:384] = gather_up(shift_one_grad, False) + gather_up(gain_two_grad, True)
    rows1[:, :128] = gather_up(shift_two_grad, False) + gather_up(down_bias_grad, True)
    up_bias_grad = jnp.concatenate(up_bias_grads, axis=1)
    picked = jnp.where(keep, jnp.broadcast_to(up_bias_grad, (PARTS, 2048)), 0.0)
    rows1[:, 128:384] = sum(picked[:, j * 256 : (j + 1) * 256] for j in range(8))
    at = rows_of((16, 384))
    for k in range(PARTS):
        a, b = rows0[k : k + 1, :], rows1[k : k + 1, :]
        vg_out[k] = jnp.where(at == 1, a, jnp.where(at == 2, b, 0.0)).astype(BF)


def down_grad_kernel(idx, mine, other, even, odd, send):
    f, x = idx[0], idx[3]
    for pair in range(PARTS // 2):
        columns = slice(pair * 256, (pair + 1) * 256)
        made = dot_tn(mine[:, columns], mine[:, 1024:]) + dot_tn(other[:, columns], other[:, 1024:])
        made = made.astype(BF)
        for one in range(2):
            slot = f ^ (2 * pair + one)
            upper, lower = made[one * 128 : one * 128 + 64], made[one * 128 + 64 : one * 128 + 128]
            kept, gone = jnp.where(x == 0, upper, lower), jnp.where(x == 0, lower, upper)
            odd_slot = slot & 1
            send[odd_slot * 4 + (slot >> 1)] = gone

            @pl.when(odd_slot == 0)
            def _():
                even[slot >> 1] = kept

            @pl.when(odd_slot == 1)
            def _():
                odd[slot >> 1] = kept


def up_grad_kernel(idx, mine, other, even, odd):
    f = idx[0]
    for pair in range(PARTS // 2):
        columns = slice(1280 + pair * 128, 1280 + (pair + 1) * 128)
        made_up = dot_tn(mine[:, columns], mine[:, :1024]) + dot_tn(other[:, columns], other[:, :1024])
        columns = slice(1792 + pair * 128, 1792 + (pair + 1) * 128)
        made_out = dot_tn(mine[:, columns], mine[:, 1024:1280]) + dot_tn(
            other[:, columns], other[:, 1024:1280]
        )
        for one in range(2):
            slot = f ^ (2 * pair + one)
            for parity, to in ((0, even), (1, odd)):

                @pl.when((slot & 1) == parity)
                def _():
                    to[slot >> 1, :, :1024] = made_up[one * 64 : (one + 1) * 64].astype(BF)
                    to[slot >> 1, :, 1024:] = made_out[one * 64 : (one + 1) * 64].astype(BF)


def attend_back_kernel(idx, *refs):
    ems, qa, ka, v, m, rinv = refs[:4], refs[4], refs[5], refs[6], refs[7], refs[8]
    xs, even, odd, vg = refs[9:13], *refs[13:16]
    dx_keep, dx_send, w_out = refs[16:19]
    weight, em_s, ema, va, eq_s, e_s = refs[19:]
    f, s = idx[0], idx[1]
    part = ems[0].shape[0]
    total = v.shape[0]
    count = total // part
    load_heads(idx, even, odd, weight)
    for k, ref in enumerate(ems):
        em_s[pl.ds(pl.multiple_of((s ^ k) * part, part), part), :] = ref[...]
    lane = lanes_of((total, 128))
    low = lane < 64
    inverse = rinv[...]
    em = em_s[...].astype(F32)
    scaled = em * inverse
    product = scaled * m[...].astype(F32)
    values = v[...]
    for h in range(2):
        mine = low if h == 0 else ~low
        delta = jnp.sum(jnp.where(mine, product, 0.0), axis=-1, keepdims=True)
        high = delta.astype(BF).astype(F32)
        at = lane - (64 if h == 0 else 0)
        extra = jnp.where(at == 0, -high, jnp.where(at == 1, high - delta, 0.0))
        ema[h] = jnp.where(mine, scaled, extra).astype(BF)
        ones = jnp.where((at == 0) | (at == 1), 1.0, 0.0)
        va[h] = jnp.where(mine, values.astype(F32), ones).astype(BF)
    lane = lanes_of((part, 128))
    low = lane < 64
    eq_s[...] = jnp.zeros_like(eq_s)
    for j in range(count):
        rows = slice(j * part, (j + 1) * part)
        start = max(j - 1, 0) * part
        grad_keys, grad_values = [], []
        for h in range(2):
            raised = jnp.exp(dot_nt(ka[h, rows, :], qa[h, start:, :]))
            slopes = dot_nt(va[h, rows, :], ema[h, start:, :])
            grad = (raised * slopes).astype(BF)
            grad_keys.append(dot_nn(grad, qa[h, start:, :]))
            grad_values.append(dot_nn(raised.astype(BF), ema[h, start:, :]))
            eq_s[h, start:, :] += dot_tn(grad, ka[h, rows, :])
        e_s[rows, 128:256] = jnp.where(low, grad_keys[0], grad_keys[1]).astype(BF)
        e_s[rows, 256:384] = jnp.where(low, grad_values[0], grad_values[1]).astype(BF)
    lane = lanes_of((total, 128))
    e_s[:, :128] = (jnp.where(lane < 64, eq_s[0], eq_s[1]) * (1.0 / math.sqrt(64))).astype(BF)
    wg = jnp.zeros(weight.shape, F32)
    for k in range(4):
        grads = e_s[pl.ds(pl.multiple_of((s ^ k) * part, part), part), :]
        wg = wg + dot_tn(xs[k][-part:, :], grads)
        made = dot_nt(grads, weight[...]).astype(BF)
        if k & 1:
            dx_send[k >> 1] = made
        else:
            dx_keep[k >> 1] = made
    bias = column_sum(e_s[...])
    at = rows_of((16, 384))
    middle = (lanes_of((16, 384)) >= 128) & (lanes_of((16, 384)) < 256)
    bias = jnp.where((at == 0) & ~middle, jnp.broadcast_to(bias, (16, 384)), 0.0)
    for k in range(PARTS):
        w_out[k, :64, :] = wg[k * 64 : (k + 1) * 64].astype(BF)
        w_out[k, 64:80, :] = (vg[k].astype(F32) + bias).astype(BF)


def plus(*terms):
    return functools.reduce(jnp.add, [t.astype(F32) for t in terms]).astype(BF)


def end_wide_kernel(idx, a, b, c, d, *refs):
    parts, (out_grad, up_grad, down_grad) = refs[:4], refs[4:]
    core, x = idx[2], idx[3]
    own = a[...].astype(F32) + c[...].astype(F32)
    other = b[...].astype(F32) + d[...].astype(F32)
    left, right = jnp.where(core == 0, own, other), jnp.where(core == 0, other, own)
    up_grad[:, :1024], up_grad[:, 1024:] = left[:, :1024], right[:, :1024]
    out_grad[:, :256], out_grad[:, 256:] = left[:, 1024:], right[:, 1024:]
    for k, ref in enumerate(parts):
        at = (core ^ (k & 1)) * 128 + (x ^ (k >> 1)) * 64
        down_grad[pl.ds(pl.multiple_of(at, 64), 64), :] = ref[...].astype(F32)


def end_heads_kernel(idx, a, b, c, d, wq, wk, wv, qb, vb, ob, g1, s1, g2, s2, db, ub):
    f, s = idx[0], idx[1]
    refs = (a, b, c, d)
    for k, ref in enumerate(refs):
        columns = pl.ds(pl.multiple_of((s ^ k) * 128, 128), 128)
        for i, to in enumerate((wq, wk, wv)):
            to[:, columns] = ref[:64, i * 128 : (i + 1) * 128].astype(F32)
    tails = [ref[64:80, :].astype(F32) for ref in refs]
    summed = (tails[0] + tails[2]) + (tails[1] + tails[3])
    bias = jnp.zeros((1, 384), F32)
    for k in range(4):
        bias = bias + jnp.where((s ^ k) == f // 2, tails[k][0:1], 0.0)
    odd = (f & 1) == 1
    for to, row in ((qb, bias[:, :128]), (vb, bias[:, 256:384])):
        to[...] = jnp.where(odd, half_roll(row), row)[:, :64].reshape(64)
    for k, to in enumerate((ob, g1, s1, g2, s2, db)):
        row, at = (summed[1:2], k + 2) if k < 4 else (summed[2:3], k - 4)
        to[...] = row[:, at * 64 : (at + 1) * 64].reshape(64)
    ub[...] = summed[2:3, 128:384].reshape(256)


COSTS.update(
    {
        attend_kernel: 0.5,
        middle_kernel: 10.2,
        down_grad_kernel: 3.4,
        up_grad_kernel: 4.0,
        attend_back_kernel: 9.3,
    }
)


def after(values, *others):
    return lax.optimization_barrier((values, *others))[0]


def swap(values, axis, step):
    size = lax.axis_size(axis)
    return lax.ppermute(values, axis, [(i, i ^ step) for i in range(size)])


def body(
    inputs,
    block_ids,
    query_weight,
    query_bias,
    key_weight,
    value_weight,
    value_bias,
    out_weight,
    out_bias,
    gain_one,
    shift_one,
    up_weight,
    up_bias,
    down_weight,
    down_bias,
    gain_two,
    shift_two,
    cotangent,
):
    owners = lax.axis_size("fsdp")
    direct = owners == PARTS
    seq = lax.axis_index("seq").astype(jnp.int32)
    fsdp = lax.axis_index("fsdp").astype(jnp.int32)
    zero = jnp.zeros((), jnp.int32)
    index = jnp.stack([fsdp if direct else zero, seq, seq & 1, seq >> 1])
    _, part, width = inputs.shape
    own = inputs.reshape(part, width)
    total = part * lax.axis_size("seq")
    vectors = (query_bias, value_bias, out_bias, gain_one, shift_one, gain_two, shift_two, down_bias)

    if direct:
        first_part, down_part = run(
            pack_kernel,
            [((80, 896), BF), ((128, 512), BF)],
            index,
            (
                query_weight,
                key_weight,
                value_weight,
                out_weight,
                up_weight,
                down_weight,
                *vectors,
                up_bias,
            ),
            scratch=(((16, 384), F32),),
            room=60,
        )
        def along_z(piece):
            return [piece] + [swap(piece, "fsdp", k) for k in (2, 4, 6)]

        mine = along_z(first_part)
        down_part = after(down_part, mine[1])
        even = jnp.stack(mine)
        odd = swap(even, "fsdp", 1)
        shared = jnp.concatenate([even[:, :, 384:].reshape(320, 512), own])
        across = swap(shared, "seq", 2)
        evens = [swap(shared, "seq", 1), across, swap(after(across, odd), "seq", 1)]
        xs = [own, *evens]
        down_even = jnp.stack(along_z(down_part))
        down_odd = swap(down_even, "fsdp", 1)
        odd_wide = odd[:, :, 384:]
        odd_across = swap(odd_wide, "seq", 2)
        odds = [swap(odd_wide, "seq", 1), odd_across]
    else:

        def full(values):
            return lax.all_gather(values, "fsdp", axis=0, tiled=True)

        vec = jnp.concatenate([full(v).reshape(PARTS, 64) for v in vectors] + [full(up_bias).reshape(PARTS, 256)], axis=1)
        vec = jnp.pad(vec.reshape(PARTS, 2, 384), ((0, 0), (0, 14), (0, 0)))
        cut = [
            lax.dynamic_slice_in_dim(full(w), seq * 128, 128, 1)
            for w in (query_weight, key_weight, value_weight)
        ]
        across = swap(own, "seq", 2)
        xs = [own, swap(own, "seq", 1), across, swap(across, "seq", 1)]
        heads = jnp.concatenate([jnp.concatenate(cut, axis=1).reshape(PARTS, 64, 384), vec], axis=1)
        core, x = seq & 1, seq >> 1
        wide = jnp.concatenate([full(out_weight), full(up_weight)], axis=1).reshape(PARTS, 64, 5, 512)
        blocks = []
        for k in range(4):
            at = (core ^ (k & 1)) * 32 + (x ^ (k >> 1)) * 16
            block = lax.dynamic_slice_in_dim(wide, at, 16, 1)
            blocks.append(block.transpose(0, 2, 1, 3).reshape(4, 2, 80, 512))
        both = jnp.concatenate([heads.reshape(4, 2, 80, 384), blocks[0]], axis=-1)
        even, odd = both[:, 0], both[:, 1]
        evens = [b[:, 0].reshape(320, 512) for b in blocks[1:]]
        odds = [b[:, 1] for b in blocks[1:]]
        tall = full(down_weight).reshape(4, 2, 256, 512)
        downs = []
        for k in range(4):
            downs.append(lax.dynamic_slice_in_dim(tall[:, k & 1], (core ^ (k >> 1)) * 128, 128, 1))

    piece = ((part, 128), BF)
    *ms, qa, ka, v, m_heads, rinv = run(
        attend_kernel,
        [piece] * 4
        + [((2, total, 128), BF)] * 2
        + [((total, 128), BF)] * 2
        + [((total, 128), F32)],
        index,
        (*xs, even, odd, block_ids),
        scratch=(
            ((512, 384), BF),
            ((PARTS, 384), F32),
            ((PARTS, 384), F32),
            ((total, 128), BF),
            ((total, 128), BF),
        ),
    )
    made = ms[0]
    ms = [made] + [swap(ms[k], "seq", k) for k in (1, 2, 3)]
    if direct:
        odds.append(swap(after(odd_across, made), "seq", 1))
        downs = [down_even, down_odd, swap(down_even, "seq", 1)]
        downs.append(swap(after(down_odd, ms[2], ms[3]), "seq", 1))
    result, *rest = run(
        middle_kernel,
        [((part, width), BF)]
        + [piece] * 4
        + [((part, width), F32)]
        + [((part, 1536), BF)] * 2
        + [((part, 2304), BF)] * 2
        + [((PARTS, 16, 384), BF)],
        index,
        (own, *ms, cotangent.reshape(part, width), even, odd, *evens, *odds, *downs),
        scratch=(
            ((512, 512), BF),
            ((512, 2048), BF),
            ((2048, 512), BF),
            ((PARTS, 384), F32),
            ((PARTS, 384), F32),
            ((part, 2048), F32),
            ((part, width), BF),
            ((part, width), BF),
            ((2, part, 1024), BF),
            ((2, part, 1024), BF),
            ((2, part, 256), BF),
            ((PARTS, 384), F32),
            ((PARTS, 384), F32),
        ),
    )
    ems, (e1, keep1, ship1, keep2, ship2, vg) = rest[:4], rest[4:]
    ems = [ems[0]] + [swap(ems[k], "seq", k) for k in (1, 2, 3)]
    up_even_grad, up_odd_grad = run(
        up_grad_kernel, [((4, 64, 1280), BF)] * 2, index, (keep2, swap(ship2, "seq", 1))
    )
    down_even, down_odd, down_send = run(
        down_grad_kernel,
        [((4, 64, 512), BF)] * 2 + [((8, 64, 512), BF)],
        index,
        (after(keep1, up_even_grad), swap(ship1, "seq", 1)),
    )
    dx_keep, dx_send, w_grad = run(
        attend_back_kernel,
        [((2, part, width), BF)] * 2 + [((PARTS, 80, 384), BF)],
        index,
        (*ems, after(qa, down_even), ka, v, m_heads, rinv, *xs, even, odd, vg),
        scratch=(
            ((512, 384), BF),
            ((total, 128), BF),
            ((2, total, 128), BF),
            ((2, total, 128), BF),
            ((2, total, 128), F32),
            ((total, 384), BF),
        ),
    )

    down_got = swap(down_send, "seq", 2)
    dx_send, down_got = lax.optimization_barrier((dx_send, down_got))
    got = swap(dx_send, "seq", 1)
    if direct:
        up_got = swap(up_odd_grad, "fsdp", 1)
        dx_keep, up_got = lax.optimization_barrier((dx_keep, up_got))
    far = swap(plus(dx_keep[1], got[1]), "seq", 2)
    input_grad = e1 + ((dx_keep[0].astype(F32) + got[0].astype(F32)) + far.astype(F32))

    if direct:

        def spread_out(mine):
            across = swap(mine, "seq", 2)
            return mine, swap(mine, "seq", 1), across, swap(across, "seq", 1)

        def cross(values):
            return [swap(values[k >> 1], "fsdp", k) for k in (2, 4, 6)]

        up_sums = [plus(up_even_grad[k], up_got[k]) for k in range(4)]
        down_got = after(down_got, dx_send)
        down_far = swap(plus(down_odd, down_got[4:]), "fsdp", 1)
        down_stay = plus(down_even, down_got[:4])
        down_far = after(down_far, *up_sums, far)
        down_sums = [plus(down_stay[k], down_far[k]) for k in range(4)]
        up_far = cross(up_sums)
        down_far = cross(down_sums)
        w_made = after(lax.all_to_all(w_grad, "fsdp", 0, 0, tiled=True), *down_sums)
        w_made = jnp.sum(w_made.astype(F32), axis=0).astype(BF)
        w_all = spread_out(w_made)
        up_all = spread_out(plus(up_sums[0], *up_far))
        down_all = spread_out(plus(down_sums[0], *down_far))
        (
            wq_grad,
            wk_grad,
            wv_grad,
            qb_grad,
            vb_grad,
            ob_grad,
            g1_grad,
            s1_grad,
            g2_grad,
            s2_grad,
            db_grad,
            ub_grad,
        ) = run(
            end_heads_kernel,
            [((64, 512), F32)] * 3 + [((64,), F32)] * 8 + [((256,), F32)],
            index,
            w_all,
        )
        out_grad, up_grad, down_grad = run(
            end_wide_kernel,
            [((64, 512), F32), ((64, 2048), F32), ((256, 512), F32)],
            index,
            up_all + down_all,
        )
    else:

        def summed(values):
            values = lax.psum_scatter(values, "fsdp", scatter_dimension=0, tiled=True)
            return lax.psum(values.astype(BF), "seq").astype(F32)

        kept = [plus(down_even, down_got[:4]), plus(down_odd, down_got[4:])]
        kept = lax.all_gather(jnp.stack(kept, axis=1).reshape(PARTS, 64, 512), "seq", axis=0)
        kept = kept.reshape(2, 2, PARTS, 64, 512).transpose(2, 1, 0, 3, 4).reshape(2048, 512)
        down_grad = lax.psum_scatter(kept.astype(F32), "fsdp", scatter_dimension=0, tiled=True)
        kept = lax.all_gather(jnp.stack([up_even_grad, up_odd_grad], axis=1).reshape(512, 1280), "seq", axis=0)
        kept = kept.astype(F32).reshape(2, 2, 512, 1280)
        kept = lax.psum_scatter(kept[0] + kept[1], "fsdp", scatter_dimension=1, tiled=True)
        up_grad = jnp.concatenate([kept[0, :, :1024], kept[1, :, :1024]], axis=1)
        out_grad = jnp.concatenate([kept[0, :, 1024:], kept[1, :, 1024:]], axis=1)
        both = w_grad.astype(F32)
        made = lax.psum_scatter(both[:, :64].reshape(512, 384), "fsdp", scatter_dimension=0, tiled=True)
        made = lax.all_gather(made.astype(BF), "seq", axis=0).astype(F32)
        wq_grad, wk_grad, wv_grad = (
            jnp.concatenate([made[t, :, i * 128 : (i + 1) * 128] for t in range(4)], axis=1)
            for i in range(3)
        )
        biases = lax.all_gather(lax.psum(both[0, 64], "fsdp").astype(BF), "seq", axis=0).astype(F32)
        cut = width // owners

        def mine(values):
            return lax.dynamic_slice_in_dim(values, fsdp * cut, cut, 0)

        qb_grad, vb_grad = mine(biases[:, :128].reshape(-1)), mine(biases[:, 256:].reshape(-1))
        flat = both[:, 65:67].reshape(PARTS, 768)
        ob_grad, g1_grad, s1_grad, g2_grad, s2_grad, db_grad = (
            summed(flat[:, k * 64 : (k + 1) * 64].reshape(-1)) for k in range(2, 8)
        )
        ub_grad = summed(flat[:, 512:].reshape(-1))

    return (
        result.reshape(inputs.shape),
        input_grad.reshape(inputs.shape),
        wq_grad,
        qb_grad,
        wk_grad,
        wv_grad,
        vb_grad,
        out_grad,
        ob_grad,
        g1_grad,
        s1_grad,
        up_grad,
        ub_grad,
        down_grad,
        db_grad,
        g2_grad,
        s2_grad,
    )


def solution(mesh):
    tokens, matrix, vector = P("fsdp", "seq", None), P("fsdp", None), P("fsdp")
    in_specs = (
        tokens,
        matrix,
        matrix,
        vector,
        matrix,
        matrix,
        vector,
        matrix,
        vector,
        vector,
        vector,
        matrix,
        vector,
        matrix,
        vector,
        vector,
        vector,
        tokens,
    )
    out_specs = (
        tokens,
        tokens,
        matrix,
        vector,
        matrix,
        matrix,
        vector,
        matrix,
        vector,
        vector,
        vector,
        matrix,
        vector,
        matrix,
        vector,
        vector,
        vector,
    )
    return jax.shard_map(body, mesh=mesh, in_specs=in_specs, out_specs=out_specs, check_vma=False)
```

```python
import functools
import math

import jax
import jax.numpy as jnp
from jax import lax
from jax.experimental import pallas as pl
from jax.experimental.pallas import tpu as pltpu
from jax.sharding import PartitionSpec as P

HEADS = 8
BLOCKS = 8
PARTS = 8
NORM_EPS = 1e-05
MASKED = -1e30
GELU_ROOT = 0.7978845608028654
GELU_CUBIC = 0.044715
BF = jnp.bfloat16
F32 = jnp.float32
COSTS = {}
VMEM = pl.BlockSpec(memory_space=pltpu.VMEM)
SMEM = pl.BlockSpec(memory_space=pltpu.SMEM)


def dot_nn(left, right):
    return lax.dot_general(left, right, (((1,), (0,)), ((), ())), preferred_element_type=F32)


def dot_nt(left, right):
    return lax.dot_general(left, right, (((1,), (1,)), ((), ())), preferred_element_type=F32)


def dot_tn(left, right):
    return lax.dot_general(left, right, (((0,), (0,)), ((), ())), preferred_element_type=F32)


def run(kernel, outs, index, args, scratch=(), room=20):
    cost = COSTS.get(kernel, 1.7)
    outs = [jax.ShapeDtypeStruct(*o) for o in outs]
    return pl.pallas_call(
        kernel,
        out_shape=outs,
        in_specs=[SMEM] + [VMEM] * len(args),
        out_specs=[VMEM] * len(outs),
        scratch_shapes=[pltpu.VMEM(*s) for s in scratch],
        compiler_params=pltpu.CompilerParams(vmem_limit_bytes=room * 1024 * 1024),
        cost_estimate=pl.CostEstimate(flops=int(cost * 1e9), bytes_accessed=int(cost * 3e6), transcendentals=0),
    )(index, *args)


def lanes_of(shape):
    return lax.broadcasted_iota(jnp.int32, shape, len(shape) - 1)


def rows_of(shape):
    return lax.broadcasted_iota(jnp.int32, shape, len(shape) - 2)


def half_roll(values):
    return pltpu.roll(values, 64, 1)


def pack_kernel(idx, wq, wk, wv, wo, up, down, *refs):
    vectors, first_out, down_out, tail = refs[:9], *refs[9:]
    s, c, x = idx[1], idx[2], idx[3]
    columns = pl.ds(pl.multiple_of(s * 128, 128), 128)
    for i, ref in enumerate((wq, wk, wv)):
        first_out[:64, i * 128 : (i + 1) * 128] = ref[:, columns]
    tail[...] = jnp.zeros_like(tail)
    for k, ref in enumerate(vectors[:8]):
        tail[k // 6 : k // 6 + 1, (k % 6) * 64 : (k % 6 + 1) * 64] = ref[...].astype(F32).reshape(1, 64)
    tail[1:2, 128:384] = vectors[8][...].astype(F32).reshape(1, 256)
    first_out[64:80, :384] = tail[...].astype(BF)
    rows = pl.ds(pl.multiple_of(c * 32 + x * 16, 16), 16)
    first_out[:16, 384:] = wo[rows, :]
    for j in range(4):
        first_out[(j + 1) * 16 : (j + 2) * 16, 384:] = up[rows, j * 512 : (j + 1) * 512]
    down_out[...] = down[pl.ds(pl.multiple_of(c * 128, 128), 128), :]


def load_vectors(idx, even, odd, first, second):
    for k in range(PARTS):
        rows = (odd if k & 1 else even)[k >> 1, 64:80, :384].astype(F32)
        first[pl.ds(idx[0] ^ k, 1), :] = rows[0:1]
        second[pl.ds(idx[0] ^ k, 1), :] = rows[1:2]


def load_heads(idx, even, odd, weight):
    for k in range(PARTS):
        rows = pl.ds(pl.multiple_of((idx[0] ^ k) * 64, 64), 64)
        weight[rows, :] = (odd if k & 1 else even)[k >> 1, :64, :384]


def key_limit(i, part, count):
    return min((i + 2) * part, count * part)


def attend_kernel(idx, *refs):
    xs, even, odd, ids = refs[:4], *refs[4:7]
    ms = refs[7:11]
    qa, ka, v_out, m_out, rinv_out = refs[11:16]
    weight, first, second, q_s, k_s = refs[16:]
    s = idx[1]
    part = ms[0].shape[0]
    count = ids.shape[1] // part
    total = part * count
    load_heads(idx, even, odd, weight)
    load_vectors(idx, even, odd, first, second)
    left, right = first[pl.ds(2 * s, 1), :][:, :128], first[pl.ds(2 * s + 1, 1), :][:, :128]
    low_row = lanes_of((1, 128)) < 64
    query_bias = jnp.where(low_row, left, half_roll(right))
    value_bias = jnp.where(low_row, half_roll(left), right)
    for k, ref in enumerate(xs):
        rows = pl.ds(pl.multiple_of((s ^ k) * part, part), part)
        made = dot_nn(ref[-part:, :], weight[...])
        q_s[rows, :] = (made[:, :128] + query_bias).astype(BF)
        k_s[rows, :] = made[:, 128:256].astype(BF)
        v_out[rows, :] = (made[:, 256:] + value_bias).astype(BF)
    blocks = jnp.broadcast_to(ids[...], (128, total))
    row = rows_of((128, total))
    row = jnp.where(row >= 64, row - 64, row)
    own = jnp.where((row < BLOCKS) & (blocks == row), 1.0, 0.0).astype(F32).T
    barred = jnp.where(
        row < BLOCKS,
        jnp.where(blocks > row, MASKED, 0.0),
        jnp.where(row < BLOCKS + 3, 1.0, 0.0),
    ).astype(F32).T
    lane = lanes_of((total, 128))
    low = lane < 64
    queries = q_s[...].astype(F32) * (1.0 / math.sqrt(64))
    keys = k_s[...].astype(F32)
    qa[0] = jnp.where(low, queries, own).astype(BF)
    qa[1] = jnp.where(low, own, queries).astype(BF)
    ka[0] = jnp.where(low, keys, barred).astype(BF)
    ka[1] = jnp.where(low, barred, keys).astype(BF)
    lane = lanes_of((part, 128))
    low = lane < 64
    for i in range(count):
        rows = slice(i * part, (i + 1) * part)
        limit = key_limit(i, part, count)
        mixed = []
        sums = []
        for h in range(2):
            scores = dot_nt(qa[h, rows, :], ka[h, :limit, :])
            top = jnp.max(scores, axis=-1, keepdims=True)
            raised = jnp.exp(scores - top).astype(BF)
            values = v_out[:limit, :]
            mine = lanes_of(values.shape) < 64
            values = jnp.where(mine if h == 0 else ~mine, values, jnp.ones_like(values))
            made = dot_nn(raised, values)
            sums.append(1.0 / half_roll(made))
            mixed.append(made * sums[-1])
            high = top.astype(BF).astype(F32)
            middle = (top - high).astype(BF).astype(F32)
            rest = top - high - middle
            at = lane - (64 if h == 0 else 0) - BLOCKS
            tops = jnp.where(at == 0, -high, jnp.where(at == 1, -middle, jnp.where(at == 2, -rest, 0.0)))
            held = qa[h, rows, :].astype(F32)
            qa[h, rows, :] = jnp.where((at >= 0) & (at < 3), tops, held).astype(BF)
        m_out[rows, :] = jnp.where(low, mixed[0], mixed[1]).astype(BF)
        rinv_out[rows, :] = jnp.where(low, sums[0], sums[1])
    for k, ref in enumerate(ms):
        ref[...] = m_out[pl.ds(pl.multiple_of((s ^ k) * part, part), part), :]


def spread(block, upper, width):
    row = rows_of((PARTS, 128))
    match = (row & 1) == (1 if upper else 0)
    block = jnp.where(match, block, half_roll(block))
    tiled = jnp.concatenate([block] * (width // 128), axis=1)
    keep = lanes_of((PARTS, width)) // 64 == rows_of((PARTS, width))
    return jnp.sum(jnp.where(keep, tiled, 0.0), axis=0, keepdims=True)


def gather_up(vector, upper):
    width = vector.shape[1]
    keep = lanes_of((PARTS, width)) // 64 == rows_of((PARTS, width))
    picked = jnp.where(keep, jnp.broadcast_to(vector, (PARTS, width)), 0.0)
    block = sum(picked[:, j * 128 : (j + 1) * 128] for j in range(width // 128))
    match = (rows_of((PARTS, 128)) & 1) == (1 if upper else 0)
    return jnp.where(match, block, half_roll(block))


def normalize(summed):
    centre = summed - jnp.mean(summed, axis=-1, keepdims=True)
    inverse = lax.rsqrt(jnp.mean(centre * centre, axis=-1, keepdims=True) + NORM_EPS)
    return centre * inverse, inverse


def norm_back(grad, normed, inverse):
    first_mean = jnp.mean(grad, axis=-1, keepdims=True)
    cross_mean = jnp.mean(grad * normed, axis=-1, keepdims=True)
    return inverse * (grad - first_mean - normed * cross_mean)


def gelu_and_slope(values):
    square = values * values
    tanh_part = jnp.tanh(values * (GELU_ROOT + (GELU_ROOT * GELU_CUBIC) * square))
    half = 0.5 + 0.5 * tanh_part
    bend = values * (0.5 * GELU_ROOT + (1.5 * GELU_ROOT * GELU_CUBIC) * square)
    return (values * half).astype(BF), half + bend * (1.0 - tanh_part * tanh_part)


def column_sum(values):
    return jnp.sum(values.astype(F32), axis=0, keepdims=True)


def middle_kernel(idx, *refs):
    x0, ms, cot, even, odd = refs[0], refs[1:5], *refs[5:8]
    even_parts, odd_parts, down_parts = refs[8:11], refs[11:14], refs[14:18]
    out, ems, e1_out = refs[18], refs[19:23], refs[23]
    keep1, ship1, keep2, ship2, vg_out = refs[24:29]
    wo, up, down, first, second, slopes, em_s, m_s, u_s, ez_s, ea_s, rows0, rows1 = refs[29:]
    f, s, c, x = idx[0], idx[1], idx[2], idx[3]
    for k in range(4):
        row = (c ^ (k & 1)) * 32 + (x ^ (k >> 1)) * 16
        for slot in range(PARTS):
            j = slot >> 1
            if k == 0:
                block = (odd if slot & 1 else even)[j, :, 384:]
            elif slot & 1:
                block = odd_parts[k - 1][j]
            else:
                block = even_parts[k - 1][j * 80 : (j + 1) * 80, :]
            rows = pl.ds(pl.multiple_of((f ^ slot) * 64 + row, 16), 16)
            wo[rows, :] = block[:16]
            for i in range(4):
                up[rows, i * 512 : (i + 1) * 512] = block[(i + 1) * 16 : (i + 2) * 16]
    for which in range(4):
        half = c if which < 2 else 1 - c
        for j in range(4):
            owner = f ^ (2 * j + (which & 1))
            rows = pl.ds(pl.multiple_of(owner * 256 + half * 128, 128), 128)
            down[rows, :] = down_parts[which][j]
    load_vectors(idx, even, odd, first, second)
    v0, v1 = first[...], second[...]
    out_bias = spread(v0[:, 128:256], False, 512)
    gain_one = spread(v0[:, 128:256], True, 512)
    shift_one = spread(v0[:, 256:384], False, 512)
    gain_two = spread(v0[:, 256:384], True, 512)
    shift_two = spread(v1[:, 0:128], False, 512)
    down_bias = spread(v1[:, 0:128], True, 512)
    keep = lanes_of((PARTS, 2048)) // 256 == rows_of((PARTS, 2048))
    tiled = jnp.concatenate([v1[:, 128:384]] * 8, axis=1)
    up_bias = jnp.sum(jnp.where(keep, tiled, 0.0), axis=0, keepdims=True)

    for k, ref in enumerate(ms):
        m_s[:, pl.ds(pl.multiple_of((s ^ k) * 128, 128), 128)] = ref[...]
    h1 = x0[...].astype(F32) + (dot_nn(m_s[...], wo[...]) + out_bias)
    n1, r1 = normalize(h1)
    y = (n1 * gain_one + shift_one).astype(BF)
    branch = jnp.zeros(h1.shape, F32)
    for j in range(4):
        columns = slice(j * 512, (j + 1) * 512)
        z = dot_nn(y, up[:, columns]) + up_bias[:, columns]
        u, slopes[:, columns] = gelu_and_slope(z)
        for one in range(2):
            owner = 2 * j + one
            for half in range(2):
                at = one * 256 + half * 128
                u_s[half, :, owner * 128 : (owner + 1) * 128] = u[:, at : at + 128]
        branch = branch + dot_nn(u, down[columns, :])
    n2, r2 = normalize(y.astype(F32) + (branch + down_bias))
    out[...] = (n2 * gain_two + shift_two).astype(BF)
    grad = cot[...].astype(F32)
    gain_two_grad = column_sum(grad * n2)
    shift_two_grad = column_sum(grad)
    e2 = norm_back(grad * gain_two, n2, r2)
    eb = e2.astype(BF)
    down_bias_grad = column_sum(eb)
    ey = e2
    up_bias_grads = []
    for j in range(4):
        columns = slice(j * 512, (j + 1) * 512)
        eu = dot_nt(eb, down[columns, :]).astype(BF).astype(F32)
        ez = (eu * slopes[:, columns]).astype(BF)
        ez_s[j // 2, :, (j % 2) * 512 : (j % 2 + 1) * 512] = ez
        up_bias_grads.append(column_sum(ez))
        ey = ey + dot_nt(ez, up[:, columns])
    gain_one_grad = column_sum(ey * n1)
    shift_one_grad = column_sum(ey)
    e1 = norm_back(ey * gain_one, n1, r1)
    e1_out[...] = e1
    ea = e1.astype(BF)
    ea_s[0], ea_s[1] = ea[:, :256], ea[:, 256:]
    out_bias_grad = column_sum(ea)
    em_s[...] = dot_nt(ea, wo[...]).astype(BF)
    for k, ref in enumerate(ems):
        ref[...] = em_s[:, pl.ds(pl.multiple_of((s ^ k) * 128, 128), 128)]
    for to1, to2, half in ((keep1, keep2, c), (ship1, ship2, 1 - c)):
        to1[:, :1024] = u_s[half]
        to1[:, 1024:] = eb
        to2[:, :1024] = ez_s[half]
        to2[:, 1024:1280] = ea_s[half]
        to2[:, 1280:1792] = y
        to2[:, 1792:] = m_s[...]
    rows0[:, :128] = jnp.zeros((PARTS, 128), F32)
    rows0[:, 128:256] = gather_up(out_bias_grad, False) + gather_up(gain_one_grad, True)
    rows0[:, 256:384] = gather_up(shift_one_grad, False) + gather_up(gain_two_grad, True)
    rows1[:, :128] = gather_up(shift_two_grad, False) + gather_up(down_bias_grad, True)
    up_bias_grad = jnp.concatenate(up_bias_grads, axis=1)
    picked = jnp.where(keep, jnp.broadcast_to(up_bias_grad, (PARTS, 2048)), 0.0)
    rows1[:, 128:384] = sum(picked[:, j * 256 : (j + 1) * 256] for j in range(8))
    at = rows_of((16, 384))
    for k in range(PARTS):
        a, b = rows0[k : k + 1, :], rows1[k : k + 1, :]
        vg_out[k] = jnp.where(at == 1, a, jnp.where(at == 2, b, 0.0)).astype(BF)


def down_grad_kernel(idx, mine, other, even, odd, send):
    f, x = idx[0], idx[3]
    made = dot_tn(mine[:, :1024], mine[:, 1024:]) + dot_tn(other[:, :1024], other[:, 1024:])
    made = made.astype(BF)
    for owner in range(PARTS):
        slot = f ^ owner
        upper, lower = made[owner * 128 : owner * 128 + 64], made[owner * 128 + 64 : owner * 128 + 128]
        kept, gone = jnp.where(x == 0, upper, lower), jnp.where(x == 0, lower, upper)
        odd_slot = slot & 1
        send[odd_slot * 4 + (slot >> 1)] = gone

        @pl.when(odd_slot == 0)
        def _():
            even[slot >> 1] = kept

        @pl.when(odd_slot == 1)
        def _():
            odd[slot >> 1] = kept


def up_grad_kernel(idx, mine, other, even, odd):
    f = idx[0]
    made_up = dot_tn(mine[:, 1280:1792], mine[:, :1024]) + dot_tn(other[:, 1280:1792], other[:, :1024])
    made_out = dot_tn(mine[:, 1792:], mine[:, 1024:1280]) + dot_tn(other[:, 1792:], other[:, 1024:1280])
    made_up, made_out = made_up.astype(BF), made_out.astype(BF)
    for owner in range(PARTS):
        slot = f ^ owner
        rows = slice(owner * 64, (owner + 1) * 64)
        for parity, to in ((0, even), (1, odd)):

            @pl.when((slot & 1) == parity)
            def _():
                to[slot >> 1, :, :1024] = made_up[rows]
                to[slot >> 1, :, 1024:] = made_out[rows]


def attend_back_kernel(idx, *refs):
    ems, qa, ka, v, m, rinv = refs[:4], refs[4], refs[5], refs[6], refs[7], refs[8]
    xs, even, odd, vg = refs[9:13], *refs[13:16]
    dx_keep, dx_send, w_out = refs[16:19]
    weight, em_s, ema, va, eq_s, e_s = refs[19:]
    f, s = idx[0], idx[1]
    part = ems[0].shape[0]
    total = v.shape[0]
    count = total // part
    load_heads(idx, even, odd, weight)
    for k, ref in enumerate(ems):
        em_s[pl.ds(pl.multiple_of((s ^ k) * part, part), part), :] = ref[...]
    lane = lanes_of((total, 128))
    low = lane < 64
    inverse = rinv[...]
    em = em_s[...].astype(F32)
    scaled = em * inverse
    product = scaled * m[...].astype(F32)
    values = v[...]
    for h in range(2):
        mine = low if h == 0 else ~low
        delta = jnp.sum(jnp.where(mine, product, 0.0), axis=-1, keepdims=True)
        high = delta.astype(BF).astype(F32)
        at = lane - (64 if h == 0 else 0)
        extra = jnp.where(at == 0, -high, jnp.where(at == 1, high - delta, 0.0))
        ema[h] = jnp.where(mine, scaled, extra).astype(BF)
        ones = jnp.where((at == 0) | (at == 1), 1.0, 0.0)
        va[h] = jnp.where(mine, values.astype(F32), ones).astype(BF)
    lane = lanes_of((part, 128))
    low = lane < 64
    eq_s[...] = jnp.zeros_like(eq_s)
    for j in range(count):
        rows = slice(j * part, (j + 1) * part)
        start = max(j - 1, 0) * part
        grad_keys, grad_values = [], []
        for h in range(2):
            raised = jnp.exp(dot_nt(ka[h, rows, :], qa[h, start:, :]))
            slopes = dot_nt(va[h, rows, :], ema[h, start:, :])
            grad = (raised * slopes).astype(BF)
            grad_keys.append(dot_nn(grad, qa[h, start:, :]))
            grad_values.append(dot_nn(raised.astype(BF), ema[h, start:, :]))
            eq_s[h, start:, :] += dot_tn(grad, ka[h, rows, :])
        e_s[rows, 128:256] = jnp.where(low, grad_keys[0], grad_keys[1]).astype(BF)
        e_s[rows, 256:384] = jnp.where(low, grad_values[0], grad_values[1]).astype(BF)
    lane = lanes_of((total, 128))
    e_s[:, :128] = (jnp.where(lane < 64, eq_s[0], eq_s[1]) * (1.0 / math.sqrt(64))).astype(BF)
    wg = jnp.zeros(weight.shape, F32)
    for k in range(4):
        grads = e_s[pl.ds(pl.multiple_of((s ^ k) * part, part), part), :]
        wg = wg + dot_tn(xs[k][-part:, :], grads)
        made = dot_nt(grads, weight[...]).astype(BF)
        if k & 1:
            dx_send[k >> 1] = made
        else:
            dx_keep[k >> 1] = made
    bias = column_sum(e_s[...])
    at = rows_of((16, 384))
    middle = (lanes_of((16, 384)) >= 128) & (lanes_of((16, 384)) < 256)
    bias = jnp.where((at == 0) & ~middle, jnp.broadcast_to(bias, (16, 384)), 0.0)
    for k in range(PARTS):
        w_out[k, :64, :] = wg[k * 64 : (k + 1) * 64].astype(BF)
        w_out[k, 64:80, :] = (vg[k].astype(F32) + bias).astype(BF)


def plus(*terms):
    return functools.reduce(jnp.add, [t.astype(F32) for t in terms]).astype(BF)


def end_wide_kernel(idx, a, b, c, d, *refs):
    parts, (out_grad, up_grad, down_grad) = refs[:4], refs[4:]
    core, x = idx[2], idx[3]
    own = a[...].astype(F32) + c[...].astype(F32)
    other = b[...].astype(F32) + d[...].astype(F32)
    left, right = jnp.where(core == 0, own, other), jnp.where(core == 0, other, own)
    up_grad[:, :1024], up_grad[:, 1024:] = left[:, :1024], right[:, :1024]
    out_grad[:, :256], out_grad[:, 256:] = left[:, 1024:], right[:, 1024:]
    for k, ref in enumerate(parts):
        at = (core ^ (k & 1)) * 128 + (x ^ (k >> 1)) * 64
        down_grad[pl.ds(pl.multiple_of(at, 64), 64), :] = ref[...].astype(F32)


def end_heads_kernel(idx, a, b, c, d, wq, wk, wv, qb, vb, ob, g1, s1, g2, s2, db, ub):
    f, s = idx[0], idx[1]
    refs = (a, b, c, d)
    for k, ref in enumerate(refs):
        columns = pl.ds(pl.multiple_of((s ^ k) * 128, 128), 128)
        for i, to in enumerate((wq, wk, wv)):
            to[:, columns] = ref[:64, i * 128 : (i + 1) * 128].astype(F32)
    tails = [ref[64:80, :].astype(F32) for ref in refs]
    summed = (tails[0] + tails[2]) + (tails[1] + tails[3])
    bias = jnp.zeros((1, 384), F32)
    for k in range(4):
        bias = bias + jnp.where((s ^ k) == f // 2, tails[k][0:1], 0.0)
    odd = (f & 1) == 1
    for to, row in ((qb, bias[:, :128]), (vb, bias[:, 256:384])):
        to[...] = jnp.where(odd, half_roll(row), row)[:, :64].reshape(64)
    for k, to in enumerate((ob, g1, s1, g2, s2, db)):
        row, at = (summed[1:2], k + 2) if k < 4 else (summed[2:3], k - 4)
        to[...] = row[:, at * 64 : (at + 1) * 64].reshape(64)
    ub[...] = summed[2:3, 128:384].reshape(256)


COSTS.update(
    {
        attend_kernel: 0.5,
        middle_kernel: 10.2,
        down_grad_kernel: 1.0,
        up_grad_kernel: 1.0,
        attend_back_kernel: 9.3,
    }
)


def after(values, *others):
    return lax.optimization_barrier((values, *others))[0]


def swap(values, axis, step):
    size = lax.axis_size(axis)
    return lax.ppermute(values, axis, [(i, i ^ step) for i in range(size)])


def body(
    inputs,
    block_ids,
    query_weight,
    query_bias,
    key_weight,
    value_weight,
    value_bias,
    out_weight,
    out_bias,
    gain_one,
    shift_one,
    up_weight,
    up_bias,
    down_weight,
    down_bias,
    gain_two,
    shift_two,
    cotangent,
):
    owners = lax.axis_size("fsdp")
    direct = owners == PARTS
    seq = lax.axis_index("seq").astype(jnp.int32)
    fsdp = lax.axis_index("fsdp").astype(jnp.int32)
    zero = jnp.zeros((), jnp.int32)
    index = jnp.stack([fsdp if direct else zero, seq, seq & 1, seq >> 1])
    _, part, width = inputs.shape
    own = inputs.reshape(part, width)
    total = part * lax.axis_size("seq")
    vectors = (query_bias, value_bias, out_bias, gain_one, shift_one, gain_two, shift_two, down_bias)

    if direct:
        first_part, down_part = run(
            pack_kernel,
            [((80, 896), BF), ((128, 512), BF)],
            index,
            (
                query_weight,
                key_weight,
                value_weight,
                out_weight,
                up_weight,
                down_weight,
                *vectors,
                up_bias,
            ),
            scratch=(((16, 384), F32),),
            room=60,
        )
        def along_z(piece):
            return [piece] + [swap(piece, "fsdp", k) for k in (2, 4, 6)]

        mine = along_z(first_part)
        even = jnp.stack(mine)
        odd = swap(even, "fsdp", 1)
        shared = jnp.concatenate([even[:, :, 384:].reshape(320, 512), own])
        across = swap(shared, "seq", 2)
        evens = [swap(shared, "seq", 1), across, swap(after(across, odd), "seq", 1)]
        xs = [own, *evens]
        down_even = jnp.stack(along_z(down_part))
        down_odd = swap(down_even, "fsdp", 1)
        odd_wide = odd[:, :, 384:]
        odd_across = swap(odd_wide, "seq", 2)
        odds = [swap(odd_wide, "seq", 1), odd_across]
    else:

        def full(values):
            return lax.all_gather(values, "fsdp", axis=0, tiled=True)

        vec = jnp.concatenate([full(v).reshape(PARTS, 64) for v in vectors] + [full(up_bias).reshape(PARTS, 256)], axis=1)
        vec = jnp.pad(vec.reshape(PARTS, 2, 384), ((0, 0), (0, 14), (0, 0)))
        cut = [
            lax.dynamic_slice_in_dim(full(w), seq * 128, 128, 1)
            for w in (query_weight, key_weight, value_weight)
        ]
        across = swap(own, "seq", 2)
        xs = [own, swap(own, "seq", 1), across, swap(across, "seq", 1)]
        heads = jnp.concatenate([jnp.concatenate(cut, axis=1).reshape(PARTS, 64, 384), vec], axis=1)
        core, x = seq & 1, seq >> 1
        wide = jnp.concatenate([full(out_weight), full(up_weight)], axis=1).reshape(PARTS, 64, 5, 512)
        blocks = []
        for k in range(4):
            at = (core ^ (k & 1)) * 32 + (x ^ (k >> 1)) * 16
            block = lax.dynamic_slice_in_dim(wide, at, 16, 1)
            blocks.append(block.transpose(0, 2, 1, 3).reshape(4, 2, 80, 512))
        both = jnp.concatenate([heads.reshape(4, 2, 80, 384), blocks[0]], axis=-1)
        even, odd = both[:, 0], both[:, 1]
        evens = [b[:, 0].reshape(320, 512) for b in blocks[1:]]
        odds = [b[:, 1] for b in blocks[1:]]
        tall = full(down_weight).reshape(4, 2, 256, 512)
        downs = []
        for k in range(4):
            downs.append(lax.dynamic_slice_in_dim(tall[:, k & 1], (core ^ (k >> 1)) * 128, 128, 1))

    piece = ((part, 128), BF)
    *ms, qa, ka, v, m_heads, rinv = run(
        attend_kernel,
        [piece] * 4
        + [((2, total, 128), BF)] * 2
        + [((total, 128), BF)] * 2
        + [((total, 128), F32)],
        index,
        (*xs, even, odd, block_ids),
        scratch=(
            ((512, 384), BF),
            ((PARTS, 384), F32),
            ((PARTS, 384), F32),
            ((total, 128), BF),
            ((total, 128), BF),
        ),
    )
    made = ms[0]
    ms = [made] + [swap(ms[k], "seq", k) for k in (1, 2, 3)]
    if direct:
        odds.append(swap(after(odd_across, made), "seq", 1))
        downs = [down_even, down_odd, swap(down_even, "seq", 1)]
        downs.append(swap(after(down_odd, ms[2], ms[3]), "seq", 1))
    result, *rest = run(
        middle_kernel,
        [((part, width), BF)]
        + [piece] * 4
        + [((part, width), F32)]
        + [((part, 1536), BF)] * 2
        + [((part, 2304), BF)] * 2
        + [((PARTS, 16, 384), BF)],
        index,
        (own, *ms, cotangent.reshape(part, width), even, odd, *evens, *odds, *downs),
        scratch=(
            ((512, 512), BF),
            ((512, 2048), BF),
            ((2048, 512), BF),
            ((PARTS, 384), F32),
            ((PARTS, 384), F32),
            ((part, 2048), F32),
            ((part, width), BF),
            ((part, width), BF),
            ((2, part, 1024), BF),
            ((2, part, 1024), BF),
            ((2, part, 256), BF),
            ((PARTS, 384), F32),
            ((PARTS, 384), F32),
        ),
    )
    ems, (e1, keep1, ship1, keep2, ship2, vg) = rest[:4], rest[4:]
    ems = [ems[0]] + [swap(ems[k], "seq", k) for k in (1, 2, 3)]
    up_even_grad, up_odd_grad = run(
        up_grad_kernel, [((4, 64, 1280), BF)] * 2, index, (keep2, swap(ship2, "seq", 1))
    )
    down_even, down_odd, down_send = run(
        down_grad_kernel,
        [((4, 64, 512), BF)] * 2 + [((8, 64, 512), BF)],
        index,
        (after(keep1, up_even_grad), swap(ship1, "seq", 1)),
    )
    dx_keep, dx_send, w_grad = run(
        attend_back_kernel,
        [((2, part, width), BF)] * 2 + [((PARTS, 80, 384), BF)],
        index,
        (*ems, qa, ka, v, m_heads, rinv, *xs, even, odd, vg),
        scratch=(
            ((512, 384), BF),
            ((total, 128), BF),
            ((2, total, 128), BF),
            ((2, total, 128), BF),
            ((2, total, 128), F32),
            ((total, 384), BF),
        ),
    )

    down_got = swap(down_send, "seq", 2)
    got = swap(dx_send, "seq", 1)
    if direct:
        up_got = swap(up_odd_grad, "fsdp", 1)
        dx_keep, up_got = lax.optimization_barrier((dx_keep, up_got))
    far = swap(plus(dx_keep[1], got[1]), "seq", 2)
    input_grad = e1 + ((dx_keep[0].astype(F32) + got[0].astype(F32)) + far.astype(F32))

    if direct:

        def spread_out(mine):
            across = swap(mine, "seq", 2)
            return mine, swap(mine, "seq", 1), across, swap(across, "seq", 1)

        def near(stay, got):
            came = swap(plus(stay[1::2], got[1::2]), "fsdp", 2)
            return plus(stay[2], got[2], came[1]), (stay[0], got[0], came[0])

        down_far = swap(plus(down_odd, down_got[4:]), "fsdp", 1)
        down_stay = plus(down_even, down_got[:4])
        up_away, up_here = near(up_even_grad, after(up_got, got))
        down_far = after(down_far, far)
        down_away, down_here = near(down_stay, down_far)
        up_far = swap(up_away, "fsdp", 4)
        down_far = swap(down_away, "fsdp", 4)
        w_made = after(lax.all_to_all(w_grad, "fsdp", 0, 0, tiled=True), up_away)
        w_made = jnp.sum(w_made.astype(F32), axis=0).astype(BF)
        w_all = spread_out(w_made)
        (
            wq_grad,
            wk_grad,
            wv_grad,
            qb_grad,
            vb_grad,
            ob_grad,
            g1_grad,
            s1_grad,
            g2_grad,
            s2_grad,
            db_grad,
            ub_grad,
        ) = run(
            end_heads_kernel,
            [((64, 512), F32)] * 3 + [((64,), F32)] * 8 + [((256,), F32)],
            index,
            w_all,
        )
        up_all = spread_out(plus(*up_here, after(up_far, input_grad, w_made)))
        down_all = spread_out(plus(*down_here, down_far))
        out_grad, up_grad, down_grad = run(
            end_wide_kernel,
            [((64, 512), F32), ((64, 2048), F32), ((256, 512), F32)],
            index,
            up_all + down_all,
        )
    else:

        def summed(values):
            values = lax.psum_scatter(values, "fsdp", scatter_dimension=0, tiled=True)
            return lax.psum(values.astype(BF), "seq").astype(F32)

        kept = [plus(down_even, down_got[:4]), plus(down_odd, down_got[4:])]
        kept = lax.all_gather(jnp.stack(kept, axis=1).reshape(PARTS, 64, 512), "seq", axis=0)
        kept = kept.reshape(2, 2, PARTS, 64, 512).transpose(2, 1, 0, 3, 4).reshape(2048, 512)
        down_grad = lax.psum_scatter(kept.astype(F32), "fsdp", scatter_dimension=0, tiled=True)
        kept = lax.all_gather(jnp.stack([up_even_grad, up_odd_grad], axis=1).reshape(512, 1280), "seq", axis=0)
        kept = kept.astype(F32).reshape(2, 2, 512, 1280)
        kept = lax.psum_scatter(kept[0] + kept[1], "fsdp", scatter_dimension=1, tiled=True)
        up_grad = jnp.concatenate([kept[0, :, :1024], kept[1, :, :1024]], axis=1)
        out_grad = jnp.concatenate([kept[0, :, 1024:], kept[1, :, 1024:]], axis=1)
        both = w_grad.astype(F32)
        made = lax.psum_scatter(both[:, :64].reshape(512, 384), "fsdp", scatter_dimension=0, tiled=True)
        made = lax.all_gather(made.astype(BF), "seq", axis=0).astype(F32)
        wq_grad, wk_grad, wv_grad = (
            jnp.concatenate([made[t, :, i * 128 : (i + 1) * 128] for t in range(4)], axis=1)
            for i in range(3)
        )
        biases = lax.all_gather(lax.psum(both[0, 64], "fsdp").astype(BF), "seq", axis=0).astype(F32)
        cut = width // owners

        def mine(values):
            return lax.dynamic_slice_in_dim(values, fsdp * cut, cut, 0)

        qb_grad, vb_grad = mine(biases[:, :128].reshape(-1)), mine(biases[:, 256:].reshape(-1))
        flat = both[:, 65:67].reshape(PARTS, 768)
        ob_grad, g1_grad, s1_grad, g2_grad, s2_grad, db_grad = (
            summed(flat[:, k * 64 : (k + 1) * 64].reshape(-1)) for k in range(2, 8)
        )
        ub_grad = summed(flat[:, 512:].reshape(-1))

    return (
        result.reshape(inputs.shape),
        input_grad.reshape(inputs.shape),
        wq_grad,
        qb_grad,
        wk_grad,
        wv_grad,
        vb_grad,
        out_grad,
        ob_grad,
        g1_grad,
        s1_grad,
        up_grad,
        ub_grad,
        down_grad,
        db_grad,
        g2_grad,
        s2_grad,
    )


def solution(mesh):
    tokens, matrix, vector = P("fsdp", "seq", None), P("fsdp", None), P("fsdp")
    in_specs = (
        tokens,
        matrix,
        matrix,
        vector,
        matrix,
        matrix,
        vector,
        matrix,
        vector,
        vector,
        vector,
        matrix,
        vector,
        matrix,
        vector,
        vector,
        vector,
        tokens,
    )
    out_specs = (
        tokens,
        tokens,
        matrix,
        vector,
        matrix,
        matrix,
        vector,
        matrix,
        vector,
        vector,
        vector,
        matrix,
        vector,
        matrix,
        vector,
        vector,
        vector,
    )
    return jax.shard_map(body, mesh=mesh, in_specs=in_specs, out_specs=out_specs, check_vma=False)
```

```python
import functools
import math

import jax
import jax.numpy as jnp
from jax import lax
from jax.experimental import pallas as pl
from jax.experimental.pallas import tpu as pltpu
from jax.sharding import PartitionSpec as P

HEADS = 8
BLOCKS = 8
PARTS = 8
NORM_EPS = 1e-05
MASKED = -1e30
GELU_ROOT = 0.7978845608028654
GELU_CUBIC = 0.044715
BF = jnp.bfloat16
F32 = jnp.float32
COSTS = {}
VMEM = pl.BlockSpec(memory_space=pltpu.VMEM)
SMEM = pl.BlockSpec(memory_space=pltpu.SMEM)


def dot_nn(left, right):
    return lax.dot_general(left, right, (((1,), (0,)), ((), ())), preferred_element_type=F32)


def dot_nt(left, right):
    return lax.dot_general(left, right, (((1,), (1,)), ((), ())), preferred_element_type=F32)


def dot_tn(left, right):
    return lax.dot_general(left, right, (((0,), (0,)), ((), ())), preferred_element_type=F32)


def run(kernel, outs, index, args, scratch=(), room=20):
    cost = COSTS.get(kernel, 1.7)
    outs = [jax.ShapeDtypeStruct(*o) for o in outs]
    return pl.pallas_call(
        kernel,
        out_shape=outs,
        in_specs=[SMEM] + [VMEM] * len(args),
        out_specs=[VMEM] * len(outs),
        scratch_shapes=[pltpu.VMEM(*s) for s in scratch],
        compiler_params=pltpu.CompilerParams(vmem_limit_bytes=room * 1024 * 1024),
        cost_estimate=pl.CostEstimate(flops=int(cost * 1e9), bytes_accessed=int(cost * 3e6), transcendentals=0),
    )(index, *args)


def lanes_of(shape):
    return lax.broadcasted_iota(jnp.int32, shape, len(shape) - 1)


def rows_of(shape):
    return lax.broadcasted_iota(jnp.int32, shape, len(shape) - 2)


def half_roll(values):
    return pltpu.roll(values, 64, 1)


def pack_kernel(idx, wq, wk, wv, wo, up, down, *refs):
    vectors, first_out, down_out, tail = refs[:9], *refs[9:]
    s, c, x = idx[1], idx[2], idx[3]
    columns = pl.ds(pl.multiple_of(s * 128, 128), 128)
    for i, ref in enumerate((wq, wk, wv)):
        first_out[:64, i * 128 : (i + 1) * 128] = ref[:, columns]
    tail[...] = jnp.zeros_like(tail)
    for k, ref in enumerate(vectors[:8]):
        tail[k // 6 : k // 6 + 1, (k % 6) * 64 : (k % 6 + 1) * 64] = ref[...].astype(F32).reshape(1, 64)
    tail[1:2, 128:384] = vectors[8][...].astype(F32).reshape(1, 256)
    first_out[64:80, :384] = tail[...].astype(BF)
    rows = pl.ds(pl.multiple_of(c * 32 + x * 16, 16), 16)
    first_out[:16, 384:] = wo[rows, :]
    for j in range(4):
        first_out[(j + 1) * 16 : (j + 2) * 16, 384:] = up[rows, j * 512 : (j + 1) * 512]
    down_out[...] = down[pl.ds(pl.multiple_of(c * 128, 128), 128), :]


def load_vectors(idx, even, odd, first, second):
    for k in range(PARTS):
        rows = (odd if k & 1 else even)[k >> 1, 64:80, :384].astype(F32)
        first[pl.ds(idx[0] ^ k, 1), :] = rows[0:1]
        second[pl.ds(idx[0] ^ k, 1), :] = rows[1:2]


def load_heads(idx, even, odd, weight):
    for k in range(PARTS):
        rows = pl.ds(pl.multiple_of((idx[0] ^ k) * 64, 64), 64)
        weight[rows, :] = (odd if k & 1 else even)[k >> 1, :64, :384]


def key_limit(i, part, count):
    return min((i + 2) * part, count * part)


def attend_kernel(idx, *refs):
    xs, even, odd, ids = refs[:4], *refs[4:7]
    ms = refs[7:11]
    qa, ka, v_out, m_out, rinv_out = refs[11:16]
    weight, first, second, q_s, k_s = refs[16:]
    s = idx[1]
    part = ms[0].shape[0]
    count = ids.shape[1] // part
    total = part * count
    load_heads(idx, even, odd, weight)
    load_vectors(idx, even, odd, first, second)
    left, right = first[pl.ds(2 * s, 1), :][:, :128], first[pl.ds(2 * s + 1, 1), :][:, :128]
    low_row = lanes_of((1, 128)) < 64
    query_bias = jnp.where(low_row, left, half_roll(right))
    value_bias = jnp.where(low_row, half_roll(left), right)
    for k, ref in enumerate(xs):
        rows = pl.ds(pl.multiple_of((s ^ k) * part, part), part)
        made = dot_nn(ref[-part:, :], weight[...])
        q_s[rows, :] = (made[:, :128] + query_bias).astype(BF)
        k_s[rows, :] = made[:, 128:256].astype(BF)
        v_out[rows, :] = (made[:, 256:] + value_bias).astype(BF)
    blocks = jnp.broadcast_to(ids[...], (128, total))
    row = rows_of((128, total))
    row = jnp.where(row >= 64, row - 64, row)
    own = jnp.where((row < BLOCKS) & (blocks == row), 1.0, 0.0).astype(F32).T
    barred = jnp.where(
        row < BLOCKS,
        jnp.where(blocks > row, MASKED, 0.0),
        jnp.where(row < BLOCKS + 3, 1.0, 0.0),
    ).astype(F32).T
    lane = lanes_of((total, 128))
    low = lane < 64
    queries = q_s[...].astype(F32) * (1.0 / math.sqrt(64))
    keys = k_s[...].astype(F32)
    qa[0] = jnp.where(low, queries, own).astype(BF)
    qa[1] = jnp.where(low, own, queries).astype(BF)
    ka[0] = jnp.where(low, keys, barred).astype(BF)
    ka[1] = jnp.where(low, barred, keys).astype(BF)
    lane = lanes_of((part, 128))
    low = lane < 64
    for i in range(count):
        rows = slice(i * part, (i + 1) * part)
        limit = key_limit(i, part, count)
        mixed = []
        sums = []
        for h in range(2):
            scores = dot_nt(qa[h, rows, :], ka[h, :limit, :])
            top = jnp.max(scores, axis=-1, keepdims=True)
            raised = jnp.exp(scores - top).astype(BF)
            values = v_out[:limit, :]
            mine = lanes_of(values.shape) < 64
            values = jnp.where(mine if h == 0 else ~mine, values, jnp.ones_like(values))
            made = dot_nn(raised, values)
            sums.append(1.0 / half_roll(made))
            mixed.append(made * sums[-1])
            high = top.astype(BF).astype(F32)
            middle = (top - high).astype(BF).astype(F32)
            rest = top - high - middle
            at = lane - (64 if h == 0 else 0) - BLOCKS
            tops = jnp.where(at == 0, -high, jnp.where(at == 1, -middle, jnp.where(at == 2, -rest, 0.0)))
            held = qa[h, rows, :].astype(F32)
            qa[h, rows, :] = jnp.where((at >= 0) & (at < 3), tops, held).astype(BF)
        m_out[rows, :] = jnp.where(low, mixed[0], mixed[1]).astype(BF)
        rinv_out[rows, :] = jnp.where(low, sums[0], sums[1])
    for k, ref in enumerate(ms):
        ref[...] = m_out[pl.ds(pl.multiple_of((s ^ k) * part, part), part), :]


def spread(block, upper, width):
    row = rows_of((PARTS, 128))
    match = (row & 1) == (1 if upper else 0)
    block = jnp.where(match, block, half_roll(block))
    tiled = jnp.concatenate([block] * (width // 128), axis=1)
    keep = lanes_of((PARTS, width)) // 64 == rows_of((PARTS, width))
    return jnp.sum(jnp.where(keep, tiled, 0.0), axis=0, keepdims=True)


def gather_up(vector, upper):
    width = vector.shape[1]
    keep = lanes_of((PARTS, width)) // 64 == rows_of((PARTS, width))
    picked = jnp.where(keep, jnp.broadcast_to(vector, (PARTS, width)), 0.0)
    block = sum(picked[:, j * 128 : (j + 1) * 128] for j in range(width // 128))
    match = (rows_of((PARTS, 128)) & 1) == (1 if upper else 0)
    return jnp.where(match, block, half_roll(block))


def normalize(summed):
    centre = summed - jnp.mean(summed, axis=-1, keepdims=True)
    inverse = lax.rsqrt(jnp.mean(centre * centre, axis=-1, keepdims=True) + NORM_EPS)
    return centre * inverse, inverse


def norm_back(grad, normed, inverse):
    first_mean = jnp.mean(grad, axis=-1, keepdims=True)
    cross_mean = jnp.mean(grad * normed, axis=-1, keepdims=True)
    return inverse * (grad - first_mean - normed * cross_mean)


def gelu_and_slope(values):
    square = values * values
    tanh_part = jnp.tanh(values * (GELU_ROOT + (GELU_ROOT * GELU_CUBIC) * square))
    half = 0.5 + 0.5 * tanh_part
    bend = values * (0.5 * GELU_ROOT + (1.5 * GELU_ROOT * GELU_CUBIC) * square)
    return (values * half).astype(BF), half + bend * (1.0 - tanh_part * tanh_part)


def column_sum(values):
    return jnp.sum(values.astype(F32), axis=0, keepdims=True)


def middle_kernel(idx, *refs):
    x0, ms, cot, even, odd = refs[0], refs[1:5], *refs[5:8]
    even_parts, odd_parts, down_parts = refs[8:11], refs[11:14], refs[14:18]
    out, ems, e1_out = refs[18], refs[19:23], refs[23]
    keep1, ship1, keep2, ship2, vg_out = refs[24:29]
    wo, up, down, first, second, slopes, em_s, m_s, u_s, ez_s, ea_s, rows0, rows1 = refs[29:]
    f, s, c, x = idx[0], idx[1], idx[2], idx[3]
    for k in range(4):
        row = (c ^ (k & 1)) * 32 + (x ^ (k >> 1)) * 16
        for slot in range(PARTS):
            j = slot >> 1
            if k == 0:
                block = (odd if slot & 1 else even)[j, :, 384:]
            elif slot & 1:
                block = odd_parts[k - 1][j]
            else:
                block = even_parts[k - 1][j * 80 : (j + 1) * 80, :]
            rows = pl.ds(pl.multiple_of((f ^ slot) * 64 + row, 16), 16)
            wo[rows, :] = block[:16]
            for i in range(4):
                up[rows, i * 512 : (i + 1) * 512] = block[(i + 1) * 16 : (i + 2) * 16]
    for which in range(4):
        half = c if which < 2 else 1 - c
        for j in range(4):
            owner = f ^ (2 * j + (which & 1))
            rows = pl.ds(pl.multiple_of(owner * 256 + half * 128, 128), 128)
            down[rows, :] = down_parts[which][j]
    load_vectors(idx, even, odd, first, second)
    v0, v1 = first[...], second[...]
    out_bias = spread(v0[:, 128:256], False, 512)
    gain_one = spread(v0[:, 128:256], True, 512)
    shift_one = spread(v0[:, 256:384], False, 512)
    gain_two = spread(v0[:, 256:384], True, 512)
    shift_two = spread(v1[:, 0:128], False, 512)
    down_bias = spread(v1[:, 0:128], True, 512)
    keep = lanes_of((PARTS, 2048)) // 256 == rows_of((PARTS, 2048))
    tiled = jnp.concatenate([v1[:, 128:384]] * 8, axis=1)
    up_bias = jnp.sum(jnp.where(keep, tiled, 0.0), axis=0, keepdims=True)

    for k, ref in enumerate(ms):
        m_s[:, pl.ds(pl.multiple_of((s ^ k) * 128, 128), 128)] = ref[...]
    h1 = x0[...].astype(F32) + (dot_nn(m_s[...], wo[...]) + out_bias)
    n1, r1 = normalize(h1)
    y = (n1 * gain_one + shift_one).astype(BF)
    branch = jnp.zeros(h1.shape, F32)
    for j in range(4):
        columns = slice(j * 512, (j + 1) * 512)
        z = dot_nn(y, up[:, columns]) + up_bias[:, columns]
        u, slopes[:, columns] = gelu_and_slope(z)
        for one in range(2):
            owner = 2 * j + one
            for half in range(2):
                at = one * 256 + half * 128
                u_s[half, :, owner * 128 : (owner + 1) * 128] = u[:, at : at + 128]
        branch = branch + dot_nn(u, down[columns, :])
    n2, r2 = normalize(y.astype(F32) + (branch + down_bias))
    out[...] = (n2 * gain_two + shift_two).astype(BF)
    grad = cot[...].astype(F32)
    gain_two_grad = column_sum(grad * n2)
    shift_two_grad = column_sum(grad)
    e2 = norm_back(grad * gain_two, n2, r2)
    eb = e2.astype(BF)
    down_bias_grad = column_sum(eb)
    ey = e2
    up_bias_grads = []
    for j in range(4):
        columns = slice(j * 512, (j + 1) * 512)
        eu = dot_nt(eb, down[columns, :]).astype(BF).astype(F32)
        ez = (eu * slopes[:, columns]).astype(BF)
        ez_s[j // 2, :, (j % 2) * 512 : (j % 2 + 1) * 512] = ez
        up_bias_grads.append(column_sum(ez))
        ey = ey + dot_nt(ez, up[:, columns])
    gain_one_grad = column_sum(ey * n1)
    shift_one_grad = column_sum(ey)
    e1 = norm_back(ey * gain_one, n1, r1)
    e1_out[...] = e1
    ea = e1.astype(BF)
    ea_s[0], ea_s[1] = ea[:, :256], ea[:, 256:]
    out_bias_grad = column_sum(ea)
    em_s[...] = dot_nt(ea, wo[...]).astype(BF)
    for k, ref in enumerate(ems):
        ref[...] = em_s[:, pl.ds(pl.multiple_of((s ^ k) * 128, 128), 128)]
    for to1, to2, half in ((keep1, keep2, c), (ship1, ship2, 1 - c)):
        to1[:, :1024] = u_s[half]
        to1[:, 1024:] = eb
        to2[:, :1024] = ez_s[half]
        to2[:, 1024:1280] = ea_s[half]
        to2[:, 1280:1792] = y
        to2[:, 1792:] = m_s[...]
    rows0[:, :128] = jnp.zeros((PARTS, 128), F32)
    rows0[:, 128:256] = gather_up(out_bias_grad, False) + gather_up(gain_one_grad, True)
    rows0[:, 256:384] = gather_up(shift_one_grad, False) + gather_up(gain_two_grad, True)
    rows1[:, :128] = gather_up(shift_two_grad, False) + gather_up(down_bias_grad, True)
    up_bias_grad = jnp.concatenate(up_bias_grads, axis=1)
    picked = jnp.where(keep, jnp.broadcast_to(up_bias_grad, (PARTS, 2048)), 0.0)
    rows1[:, 128:384] = sum(picked[:, j * 256 : (j + 1) * 256] for j in range(8))
    at = rows_of((16, 384))
    for k in range(PARTS):
        a, b = rows0[k : k + 1, :], rows1[k : k + 1, :]
        vg_out[k] = jnp.where(at == 1, a, jnp.where(at == 2, b, 0.0)).astype(BF)


def down_grad_kernel(idx, mine, other, even, odd, send):
    f, x = idx[0], idx[3]
    made = dot_tn(mine[:, :1024], mine[:, 1024:]) + dot_tn(other[:, :1024], other[:, 1024:])
    made = made.astype(BF)
    for owner in range(PARTS):
        slot = f ^ owner
        upper, lower = made[owner * 128 : owner * 128 + 64], made[owner * 128 + 64 : owner * 128 + 128]
        kept, gone = jnp.where(x == 0, upper, lower), jnp.where(x == 0, lower, upper)
        odd_slot = slot & 1
        send[odd_slot * 4 + (slot >> 1)] = gone

        @pl.when(odd_slot == 0)
        def _():
            even[slot >> 1] = kept

        @pl.when(odd_slot == 1)
        def _():
            odd[slot >> 1] = kept


def up_grad_kernel(idx, mine, other, even, odd):
    f = idx[0]
    made_up = dot_tn(mine[:, 1280:1792], mine[:, :1024]) + dot_tn(other[:, 1280:1792], other[:, :1024])
    made_out = dot_tn(mine[:, 1792:], mine[:, 1024:1280]) + dot_tn(other[:, 1792:], other[:, 1024:1280])
    made_up, made_out = made_up.astype(BF), made_out.astype(BF)
    for owner in range(PARTS):
        slot = f ^ owner
        rows = slice(owner * 64, (owner + 1) * 64)
        for parity, to in ((0, even), (1, odd)):

            @pl.when((slot & 1) == parity)
            def _():
                to[slot >> 1, :, :1024] = made_up[rows]
                to[slot >> 1, :, 1024:] = made_out[rows]


def attend_back_kernel(idx, *refs):
    ems, qa, ka, v, m, rinv = refs[:4], refs[4], refs[5], refs[6], refs[7], refs[8]
    xs, even, odd, vg = refs[9:13], *refs[13:16]
    dx_keep, dx_send, w_out = refs[16:19]
    weight, em_s, ema, va, eq_s, e_s = refs[19:]
    f, s = idx[0], idx[1]
    part = ems[0].shape[0]
    total = v.shape[0]
    count = total // part
    load_heads(idx, even, odd, weight)
    for k, ref in enumerate(ems):
        em_s[pl.ds(pl.multiple_of((s ^ k) * part, part), part), :] = ref[...]
    lane = lanes_of((total, 128))
    low = lane < 64
    inverse = rinv[...]
    em = em_s[...].astype(F32)
    scaled = em * inverse
    product = scaled * m[...].astype(F32)
    values = v[...]
    for h in range(2):
        mine = low if h == 0 else ~low
        delta = jnp.sum(jnp.where(mine, product, 0.0), axis=-1, keepdims=True)
        high = delta.astype(BF).astype(F32)
        at = lane - (64 if h == 0 else 0)
        extra = jnp.where(at == 0, -high, jnp.where(at == 1, high - delta, 0.0))
        ema[h] = jnp.where(mine, scaled, extra).astype(BF)
        ones = jnp.where((at == 0) | (at == 1), 1.0, 0.0)
        va[h] = jnp.where(mine, values.astype(F32), ones).astype(BF)
    lane = lanes_of((part, 128))
    low = lane < 64
    eq_s[...] = jnp.zeros_like(eq_s)
    for j in range(count):
        rows = slice(j * part, (j + 1) * part)
        start = max(j - 1, 0) * part
        grad_keys, grad_values = [], []
        for h in range(2):
            raised = jnp.exp(dot_nt(ka[h, rows, :], qa[h, start:, :]))
            slopes = dot_nt(va[h, rows, :], ema[h, start:, :])
            grad = (raised * slopes).astype(BF)
            grad_keys.append(dot_nn(grad, qa[h, start:, :]))
            grad_values.append(dot_nn(raised.astype(BF), ema[h, start:, :]))
            eq_s[h, start:, :] += dot_tn(grad, ka[h, rows, :])
        e_s[rows, 128:256] = jnp.where(low, grad_keys[0], grad_keys[1]).astype(BF)
        e_s[rows, 256:384] = jnp.where(low, grad_values[0], grad_values[1]).astype(BF)
    lane = lanes_of((total, 128))
    e_s[:, :128] = (jnp.where(lane < 64, eq_s[0], eq_s[1]) * (1.0 / math.sqrt(64))).astype(BF)
    wg = jnp.zeros(weight.shape, F32)
    for k in range(4):
        grads = e_s[pl.ds(pl.multiple_of((s ^ k) * part, part), part), :]
        wg = wg + dot_tn(xs[k][-part:, :], grads)
        made = dot_nt(grads, weight[...]).astype(BF)
        if k & 1:
            dx_send[k >> 1] = made
        else:
            dx_keep[k >> 1] = made
    bias = column_sum(e_s[...])
    at = rows_of((16, 384))
    middle = (lanes_of((16, 384)) >= 128) & (lanes_of((16, 384)) < 256)
    bias = jnp.where((at == 0) & ~middle, jnp.broadcast_to(bias, (16, 384)), 0.0)
    for k in range(PARTS):
        w_out[k, :64, :] = wg[k * 64 : (k + 1) * 64].astype(BF)
        w_out[k, 64:80, :] = (vg[k].astype(F32) + bias).astype(BF)


def plus(*terms):
    return functools.reduce(jnp.add, [t.astype(F32) for t in terms]).astype(BF)


def end_wide_kernel(idx, a, b, c, d, *refs):
    parts, (out_grad, up_grad, down_grad) = refs[:4], refs[4:]
    core, x = idx[2], idx[3]
    own = a[...].astype(F32) + c[...].astype(F32)
    other = b[...].astype(F32) + d[...].astype(F32)
    left, right = jnp.where(core == 0, own, other), jnp.where(core == 0, other, own)
    up_grad[:, :1024], up_grad[:, 1024:] = left[:, :1024], right[:, :1024]
    out_grad[:, :256], out_grad[:, 256:] = left[:, 1024:], right[:, 1024:]
    for k, ref in enumerate(parts):
        at = (core ^ (k & 1)) * 128 + (x ^ (k >> 1)) * 64
        down_grad[pl.ds(pl.multiple_of(at, 64), 64), :] = ref[...].astype(F32)


def end_heads_kernel(idx, a, b, c, d, wq, wk, wv, qb, vb, ob, g1, s1, g2, s2, db, ub):
    f, s = idx[0], idx[1]
    refs = (a, b, c, d)
    for k, ref in enumerate(refs):
        columns = pl.ds(pl.multiple_of((s ^ k) * 128, 128), 128)
        for i, to in enumerate((wq, wk, wv)):
            to[:, columns] = ref[:64, i * 128 : (i + 1) * 128].astype(F32)
    tails = [ref[64:80, :].astype(F32) for ref in refs]
    summed = (tails[0] + tails[2]) + (tails[1] + tails[3])
    bias = jnp.zeros((1, 384), F32)
    for k in range(4):
        bias = bias + jnp.where((s ^ k) == f // 2, tails[k][0:1], 0.0)
    odd = (f & 1) == 1
    for to, row in ((qb, bias[:, :128]), (vb, bias[:, 256:384])):
        to[...] = jnp.where(odd, half_roll(row), row)[:, :64].reshape(64)
    for k, to in enumerate((ob, g1, s1, g2, s2, db)):
        row, at = (summed[1:2], k + 2) if k < 4 else (summed[2:3], k - 4)
        to[...] = row[:, at * 64 : (at + 1) * 64].reshape(64)
    ub[...] = summed[2:3, 128:384].reshape(256)


COSTS.update(
    {
        attend_kernel: 0.1,
        middle_kernel: 3.0,
        down_grad_kernel: 1.0,
        up_grad_kernel: 1.0,
        attend_back_kernel: 7.0,
    }
)


def after(values, *others):
    return lax.optimization_barrier((values, *others))[0]


def swap(values, axis, step):
    size = lax.axis_size(axis)
    return lax.ppermute(values, axis, [(i, i ^ step) for i in range(size)])


def body(
    inputs,
    block_ids,
    query_weight,
    query_bias,
    key_weight,
    value_weight,
    value_bias,
    out_weight,
    out_bias,
    gain_one,
    shift_one,
    up_weight,
    up_bias,
    down_weight,
    down_bias,
    gain_two,
    shift_two,
    cotangent,
):
    owners = lax.axis_size("fsdp")
    direct = owners == PARTS
    seq = lax.axis_index("seq").astype(jnp.int32)
    fsdp = lax.axis_index("fsdp").astype(jnp.int32)
    zero = jnp.zeros((), jnp.int32)
    index = jnp.stack([fsdp if direct else zero, seq, seq & 1, seq >> 1])
    _, part, width = inputs.shape
    own = inputs.reshape(part, width)
    total = part * lax.axis_size("seq")
    vectors = (query_bias, value_bias, out_bias, gain_one, shift_one, gain_two, shift_two, down_bias)

    if direct:
        first_part, down_part = run(
            pack_kernel,
            [((80, 896), BF), ((128, 512), BF)],
            index,
            (
                query_weight,
                key_weight,
                value_weight,
                out_weight,
                up_weight,
                down_weight,
                *vectors,
                up_bias,
            ),
            scratch=(((16, 384), F32),),
            room=60,
        )
        def along_z(piece):
            return [piece] + [swap(piece, "fsdp", k) for k in (2, 4, 6)]

        mine = along_z(first_part)
        even = jnp.stack(mine)
        odd = swap(even, "fsdp", 1)
        shared = jnp.concatenate([even[:, :, 384:].reshape(320, 512), own])
        across = swap(shared, "seq", 2)
        evens = [swap(shared, "seq", 1), across, swap(after(across, odd), "seq", 1)]
        xs = [own, *evens]
        down_even = jnp.stack(along_z(down_part))
        down_odd = swap(down_even, "fsdp", 1)
        odd_wide = odd[:, :, 384:]
        odd_across = swap(odd_wide, "seq", 2)
        odds = [swap(odd_wide, "seq", 1), odd_across]
    else:

        def full(values):
            return lax.all_gather(values, "fsdp", axis=0, tiled=True)

        vec = jnp.concatenate([full(v).reshape(PARTS, 64) for v in vectors] + [full(up_bias).reshape(PARTS, 256)], axis=1)
        vec = jnp.pad(vec.reshape(PARTS, 2, 384), ((0, 0), (0, 14), (0, 0)))
        cut = [
            lax.dynamic_slice_in_dim(full(w), seq * 128, 128, 1)
            for w in (query_weight, key_weight, value_weight)
        ]
        across = swap(own, "seq", 2)
        xs = [own, swap(own, "seq", 1), across, swap(across, "seq", 1)]
        heads = jnp.concatenate([jnp.concatenate(cut, axis=1).reshape(PARTS, 64, 384), vec], axis=1)
        core, x = seq & 1, seq >> 1
        wide = jnp.concatenate([full(out_weight), full(up_weight)], axis=1).reshape(PARTS, 64, 5, 512)
        blocks = []
        for k in range(4):
            at = (core ^ (k & 1)) * 32 + (x ^ (k >> 1)) * 16
            block = lax.dynamic_slice_in_dim(wide, at, 16, 1)
            blocks.append(block.transpose(0, 2, 1, 3).reshape(4, 2, 80, 512))
        both = jnp.concatenate([heads.reshape(4, 2, 80, 384), blocks[0]], axis=-1)
        even, odd = both[:, 0], both[:, 1]
        evens = [b[:, 0].reshape(320, 512) for b in blocks[1:]]
        odds = [b[:, 1] for b in blocks[1:]]
        tall = full(down_weight).reshape(4, 2, 256, 512)
        downs = []
        for k in range(4):
            downs.append(lax.dynamic_slice_in_dim(tall[:, k & 1], (core ^ (k >> 1)) * 128, 128, 1))

    piece = ((part, 128), BF)
    *ms, qa, ka, v, m_heads, rinv = run(
        attend_kernel,
        [piece] * 4
        + [((2, total, 128), BF)] * 2
        + [((total, 128), BF)] * 2
        + [((total, 128), F32)],
        index,
        (*xs, even, odd, block_ids),
        scratch=(
            ((512, 384), BF),
            ((PARTS, 384), F32),
            ((PARTS, 384), F32),
            ((total, 128), BF),
            ((total, 128), BF),
        ),
    )
    made = ms[0]
    ms = [made] + [swap(ms[k], "seq", k) for k in (1, 2, 3)]
    if direct:
        odds.append(swap(after(odd_across, made), "seq", 1))
        downs = [down_even, down_odd, swap(down_even, "seq", 1)]
        downs.append(swap(after(down_odd, ms[2], ms[3]), "seq", 1))
    result, *rest = run(
        middle_kernel,
        [((part, width), BF)]
        + [piece] * 4
        + [((part, width), F32)]
        + [((part, 1536), BF)] * 2
        + [((part, 2304), BF)] * 2
        + [((PARTS, 16, 384), BF)],
        index,
        (own, *ms, cotangent.reshape(part, width), even, odd, *evens, *odds, *downs),
        scratch=(
            ((512, 512), BF),
            ((512, 2048), BF),
            ((2048, 512), BF),
            ((PARTS, 384), F32),
            ((PARTS, 384), F32),
            ((part, 2048), F32),
            ((part, width), BF),
            ((part, width), BF),
            ((2, part, 1024), BF),
            ((2, part, 1024), BF),
            ((2, part, 256), BF),
            ((PARTS, 384), F32),
            ((PARTS, 384), F32),
        ),
    )
    ems, (e1, keep1, ship1, keep2, ship2, vg) = rest[:4], rest[4:]
    ems = [ems[0]] + [swap(ems[k], "seq", k) for k in (1, 2, 3)]
    up_even_grad, up_odd_grad = run(
        up_grad_kernel, [((4, 64, 1280), BF)] * 2, index, (keep2, swap(ship2, "seq", 1))
    )
    down_even, down_odd, down_send = run(
        down_grad_kernel,
        [((4, 64, 512), BF)] * 2 + [((8, 64, 512), BF)],
        index,
        (after(keep1, up_even_grad), swap(ship1, "seq", 1)),
    )
    dx_keep, dx_send, w_grad = run(
        attend_back_kernel,
        [((2, part, width), BF)] * 2 + [((PARTS, 80, 384), BF)],
        index,
        (*ems, qa, ka, v, m_heads, rinv, *xs, even, odd, vg),
        scratch=(
            ((512, 384), BF),
            ((total, 128), BF),
            ((2, total, 128), BF),
            ((2, total, 128), BF),
            ((2, total, 128), F32),
            ((total, 384), BF),
        ),
    )

    down_got = swap(down_send, "seq", 2)
    got = swap(dx_send, "seq", 1)
    if direct:
        up_got = swap(up_odd_grad, "fsdp", 1)
        dx_keep, up_got = lax.optimization_barrier((dx_keep, up_got))
        up_got = after(up_got, got)
        up_here, up_gone = plus(up_even_grad[::2], up_got[::2]), plus(up_even_grad[1::2], up_got[1::2])
    far = swap(plus(dx_keep[1], got[1]), "seq", 2)
    input_grad = e1 + ((dx_keep[0].astype(F32) + got[0].astype(F32)) + far.astype(F32))

    if direct:

        def spread_out(mine):
            across = swap(mine, "seq", 2)
            return mine, swap(mine, "seq", 1), across, swap(across, "seq", 1)

        down_far = swap(plus(down_odd, down_got[4:]), "fsdp", 1)
        down_stay = plus(down_even, down_got[:4])
        up_came = swap(up_gone, "fsdp", 2)
        up_away = plus(up_here[1], up_came[1])
        down_far = after(down_far, far)
        down_here = plus(down_stay[::2], down_far[::2])
        down_came = swap(plus(down_stay[1::2], down_far[1::2]), "fsdp", 2)
        down_away = plus(down_here[1], down_came[1])
        up_far = swap(up_away, "fsdp", 4)
        down_far = swap(down_away, "fsdp", 4)
        w_made = after(lax.all_to_all(w_grad, "fsdp", 0, 0, tiled=True), up_away)
        w_made = jnp.sum(w_made.astype(F32), axis=0).astype(BF)
        w_all = spread_out(w_made)
        (
            wq_grad,
            wk_grad,
            wv_grad,
            qb_grad,
            vb_grad,
            ob_grad,
            g1_grad,
            s1_grad,
            g2_grad,
            s2_grad,
            db_grad,
            ub_grad,
        ) = run(
            end_heads_kernel,
            [((64, 512), F32)] * 3 + [((64,), F32)] * 8 + [((256,), F32)],
            index,
            w_all,
        )
        up_all = spread_out(plus(up_here[0], up_came[0], after(up_far, input_grad, w_made)))
        down_all = spread_out(plus(down_here[0], down_came[0], after(down_far, up_all[0])))
        out_grad, up_grad, down_grad = run(
            end_wide_kernel,
            [((64, 512), F32), ((64, 2048), F32), ((256, 512), F32)],
            index,
            up_all + down_all,
        )
    else:

        def summed(values):
            values = lax.psum_scatter(values, "fsdp", scatter_dimension=0, tiled=True)
            return lax.psum(values.astype(BF), "seq").astype(F32)

        kept = [plus(down_even, down_got[:4]), plus(down_odd, down_got[4:])]
        kept = lax.all_gather(jnp.stack(kept, axis=1).reshape(PARTS, 64, 512), "seq", axis=0)
        kept = kept.reshape(2, 2, PARTS, 64, 512).transpose(2, 1, 0, 3, 4).reshape(2048, 512)
        down_grad = lax.psum_scatter(kept.astype(F32), "fsdp", scatter_dimension=0, tiled=True)
        kept = lax.all_gather(jnp.stack([up_even_grad, up_odd_grad], axis=1).reshape(512, 1280), "seq", axis=0)
        kept = kept.astype(F32).reshape(2, 2, 512, 1280)
        kept = lax.psum_scatter(kept[0] + kept[1], "fsdp", scatter_dimension=1, tiled=True)
        up_grad = jnp.concatenate([kept[0, :, :1024], kept[1, :, :1024]], axis=1)
        out_grad = jnp.concatenate([kept[0, :, 1024:], kept[1, :, 1024:]], axis=1)
        both = w_grad.astype(F32)
        made = lax.psum_scatter(both[:, :64].reshape(512, 384), "fsdp", scatter_dimension=0, tiled=True)
        made = lax.all_gather(made.astype(BF), "seq", axis=0).astype(F32)
        wq_grad, wk_grad, wv_grad = (
            jnp.concatenate([made[t, :, i * 128 : (i + 1) * 128] for t in range(4)], axis=1)
            for i in range(3)
        )
        biases = lax.all_gather(lax.psum(both[0, 64], "fsdp").astype(BF), "seq", axis=0).astype(F32)
        cut = width // owners

        def mine(values):
            return lax.dynamic_slice_in_dim(values, fsdp * cut, cut, 0)

        qb_grad, vb_grad = mine(biases[:, :128].reshape(-1)), mine(biases[:, 256:].reshape(-1))
        flat = both[:, 65:67].reshape(PARTS, 768)
        ob_grad, g1_grad, s1_grad, g2_grad, s2_grad, db_grad = (
            summed(flat[:, k * 64 : (k + 1) * 64].reshape(-1)) for k in range(2, 8)
        )
        ub_grad = summed(flat[:, 512:].reshape(-1))

    return (
        result.reshape(inputs.shape),
        input_grad.reshape(inputs.shape),
        wq_grad,
        qb_grad,
        wk_grad,
        wv_grad,
        vb_grad,
        out_grad,
        ob_grad,
        g1_grad,
        s1_grad,
        up_grad,
        ub_grad,
        down_grad,
        db_grad,
        g2_grad,
        s2_grad,
    )


def solution(mesh):
    tokens, matrix, vector = P("fsdp", "seq", None), P("fsdp", None), P("fsdp")
    in_specs = (
        tokens,
        matrix,
        matrix,
        vector,
        matrix,
        matrix,
        vector,
        matrix,
        vector,
        vector,
        vector,
        matrix,
        vector,
        matrix,
        vector,
        vector,
        vector,
        tokens,
    )
    out_specs = (
        tokens,
        tokens,
        matrix,
        vector,
        matrix,
        matrix,
        vector,
        matrix,
        vector,
        vector,
        vector,
        matrix,
        vector,
        matrix,
        vector,
        vector,
        vector,
    )
    return jax.shard_map(body, mesh=mesh, in_specs=in_specs, out_specs=out_specs, check_vma=False)
```
